512 devices in a mesh: lat: 16 (over y_lo, x, core), lon: 32 (over z, y_hi).
Axes of the slice: x: 4, y: 8 (y_hi: 4, y_lo: 2; y = y_hi * 2 + y_lo), z: 8, core: 2. Of those that a mesh axis runs over, the one named last changes fastest.
Arguments:
- tokens: bfloat16 [2, 96, 73728], P(None, 'lat', 'lon'), may hold values from -6 to 6
- labels: int32 [2, 96, 384], P(None, 'lat', 'lon'), may hold values from 0 to 3, as said below
- norm1_gain: float32 [192], replicated, may hold values from 0.1 to 1.9
- qkv_weight: bfloat16 [192, 576], replicated, may hold values from -0.4375 to 0.4375
- proj_weight: bfloat16 [192, 192], replicated, may hold values from -0.4375 to 0.4375
- bias_table: float32 [16, 6, 23, 144], P('lat'), may hold values from -3 to 350
- norm2_gain: float32 [192], replicated, may hold values from 0.1 to 1.9
- up_weight: bfloat16 [192, 768], replicated, may hold values from -0.4375 to 0.4375
- down_weight: bfloat16 [768, 192], replicated, may hold values from -0.21875 to 0.21875
- cotangent: bfloat16 [2, 96, 73728], P(None, 'lat', 'lon'), may hold values from -6 to 6
Outputs:
- block_out: bfloat16 [2, 96, 73728], P(None, 'lat', 'lon')
- token_grad: bfloat16 [2, 96, 73728], P(None, 'lat', 'lon')
- norm1_grad: float32 [192], replicated
- qkv_grad: float32 [192, 576], replicated
- proj_grad: float32 [192, 192], replicated
- bias_grad: float32 [16, 6, 23, 144], P('lat')
- norm2_grad: float32 [192], replicated
- up_grad: float32 [192, 768], replicated
- down_grad: float32 [768, 192], replicated
The draws below stay inside these ranges and needn't reach their ends.
Inputs may be any that keep to these rules, and one draw needn't show every extreme that they name: `labels`: A cell of the rolled frame in the last 3 latitude rows has an odd label and every other cell an even one.
All inputs are finite; a program needn't handle non-finite values.
Results may differ from the reference program's by a relative error of at most 0.023.
Values may be sent and summed in bfloat16 or wider, within the bound.
A program may use at most 64 MiB of HBM per device.

```python
import jax
import jax.numpy as jnp
from jax import lax

C = 192
HEADS = 6
FFN = 768
LEVELS = 2
LATS = 96
LONS = 384
NLATWIN = 16
TOKENS = 73728


def draw_labels(key, part):
    key = jax.random.fold_in(key, 11)
    region = jax.random.randint(key, (LEVELS, LATS, LONS), 0, 2, dtype=jnp.int32)
    lat_rows = jnp.arange(LATS, dtype=jnp.int32)[None, :, None]
    wrapped = (lat_rows >= LATS - 3).astype(jnp.int32)
    return 2 * region + wrapped


def draw_bias_table(key, part):
    key = jax.random.fold_in(key, 23)
    table_shape = (NLATWIN, HEADS, 23, 144)
    return jax.random.truncated_normal(key, -3.0, 3.0, table_shape, jnp.float32)


def block_scale(own_key, shape, split, smallest, top_value):
    level, own = 1.0, jax.random.fold_in(own_key, 6)
    for position, shards_of in split:
        heights = jnp.exp(jax.random.uniform(jax.random.fold_in(own, position), (shards_of,), jnp.float32, smallest / len(split), top_value / len(split)))
        level = level * jnp.repeat(heights, shape[position] // shards_of).reshape([-1 if axis == position else 1 for axis in range(len(shape))])
    return level


def bell_draw(rng, extent, scale, limit, pieces=(), kind=jnp.bfloat16):
    factor_of = block_scale(rng, extent, pieces, -0.22, 0.18) if pieces else 1.0
    result = jax.random.normal(rng, extent, jnp.float32) * scale * factor_of
    return jnp.minimum(jnp.maximum(result, -limit), limit).astype(kind)


def setup_inputs(seed: int = 0) -> dict:
    key_of = jax.random.split(jax.random.key(seed), 11)
    return {
        "tokens": bell_draw(key_of[0], (LEVELS, LATS, LONS * C), 1.0, 6.0, ((1, 16), (2, 32))),
        "labels": draw_labels(jax.random.fold_in(key_of[10], 71), 0),
        "norm1_gain": jnp.clip(1.0 + 0.18 * jax.random.normal(key_of[2], (C,), jnp.float32), 0.1, 1.9),
        "qkv_weight": bell_draw(key_of[3], (C, 3 * C), C ** -0.5, 0.4375),
        "proj_weight": bell_draw(key_of[4], (C, C), C ** -0.5, 0.4375),
        "bias_table": draw_bias_table(jax.random.fold_in(key_of[10], 71), 0),
        "norm2_gain": jnp.clip(1.0 + 0.18 * jax.random.normal(key_of[6], (C,), jnp.float32), 0.1, 1.9),
        "up_weight": bell_draw(key_of[7], (C, FFN), C ** -0.5, 0.4375),
        "down_weight": bell_draw(key_of[8], (FFN, C), FFN ** -0.5, 0.21875),
        "cotangent": bell_draw(key_of[9], (LEVELS, LATS, LONS * C), 1.0, 6.0, ((1, 16), (2, 32))),
    }


norm_eps = 1e-05
gelu_coeff = 0.044715
root_two_over_pi = 0.7978845608028654
masked_score = -1e+30

def layer_norm(values, gain_vec):
    center = values - lax.optimization_barrier(jnp.mean(values, axis=-1, keepdims=True))
    inv_std = lax.rsqrt(lax.optimization_barrier(jnp.mean(center * center, axis=-1, keepdims=True)) + norm_eps)
    normal_part = center * inv_std
    return (normal_part * gain_vec, normal_part, inv_std)

def norm_back(grad_out, normal_part, inv_std, gain_vec):
    scaled = grad_out * gain_vec
    grad_in = inv_std * (scaled - lax.optimization_barrier(jnp.mean(scaled, axis=-1, keepdims=True)) - normal_part * lax.optimization_barrier(jnp.mean(scaled * normal_part, axis=-1, keepdims=True)))
    return (grad_in, lax.optimization_barrier(jnp.sum(grad_out * normal_part, axis=0)))

def gelu_value(pre_act):
    tanh_part = jnp.tanh(root_two_over_pi * (pre_act + gelu_coeff * pre_act * pre_act * pre_act))
    return 0.5 * pre_act * (1.0 + tanh_part)

def gelu_slope(pre_act):
    tanh_part = jnp.tanh(root_two_over_pi * (pre_act + gelu_coeff * pre_act * pre_act * pre_act))
    return 0.5 * (1.0 + tanh_part) + 0.5 * pre_act * (1.0 - tanh_part * tanh_part) * root_two_over_pi * (1.0 + 3.0 * gelu_coeff * pre_act * pre_act)

def lon_table():
    offsets = jnp.arange(144, dtype=jnp.int32)
    spread = offsets % 12 - offsets // 12 + 11
    return (spread[:, None] == jnp.arange(23, dtype=jnp.int32)[None, :]).astype(jnp.float32)

def expand_bias(table_band):
    full_bias = jnp.einsum('hdp,ed->hpe', table_band, lon_table(), precision=lax.Precision.HIGHEST)
    head_count = full_bias.shape[0]
    full_bias = full_bias.reshape(head_count, 2, 6, 2, 6, 12, 12).transpose(0, 1, 2, 5, 3, 4, 6)
    return full_bias.reshape(head_count, 144, 144)

def fold_bias(grad_full):
    head_count = grad_full.shape[0]
    folded = grad_full.reshape(head_count, 2, 6, 12, 2, 6, 12).transpose(0, 1, 2, 4, 5, 3, 6)
    folded = folded.reshape(head_count, 144, 144)
    return jnp.einsum('hpe,ed->hdp', folded, lon_table(), precision=lax.Precision.HIGHEST)

def to_windows(frame_data):
    level_count, lat_cells, lon_cells, features = frame_data.shape
    blocks = frame_data.reshape(level_count, lat_cells // 6, 6, lon_cells // 12, 12, features)
    return blocks.transpose(1, 3, 0, 2, 4, 5).reshape(lat_cells // 6, lon_cells // 12, level_count * 72, features)

def from_windows(windows, level_count):
    lat_wins, lon_wins, window_cells, features = windows.shape
    blocks = windows.reshape(lat_wins, lon_wins, level_count, 6, 12, features).transpose(2, 0, 3, 1, 4, 5)
    return blocks.reshape(level_count, lat_wins * 6, lon_wins * 12, features)

def attend(packed, table_band, labels_band):
    lon_wins, window_cells, triple = packed.shape
    features = triple // 3
    head_size = features // HEADS
    split_parts = packed.reshape(lon_wins, window_cells, 3, HEADS, head_size).astype(jnp.float32)
    scores = jnp.einsum('bqhd,bkhd->bhqk', split_parts[:, :, 0], split_parts[:, :, 1])
    scores = scores * head_size ** (-0.5) + expand_bias(table_band)[None]
    same_label = labels_band[:, :, None] == labels_band[:, None, :]
    scores = jnp.where(same_label[:, None], scores, masked_score)
    weights = jnp.exp(scores - lax.optimization_barrier(jnp.max(scores, axis=-1, keepdims=True)))
    weights = weights / lax.optimization_barrier(jnp.sum(weights, axis=-1, keepdims=True))
    rounded = weights.astype(jnp.bfloat16).astype(jnp.float32)
    mixed_heads = jnp.einsum('bhqk,bkhd->bqhd', rounded, split_parts[:, :, 2])
    return (mixed_heads.astype(jnp.bfloat16).reshape(lon_wins, window_cells, features), weights)

def attend_back(packed, weights, grad_mixed):
    lon_wins, window_cells, triple = packed.shape
    features = triple // 3
    head_size = features // HEADS
    split_parts = packed.reshape(lon_wins, window_cells, 3, HEADS, head_size).astype(jnp.float32)
    queries, keys, values = (split_parts[:, :, 0], split_parts[:, :, 1], split_parts[:, :, 2])
    grad_heads = grad_mixed.reshape(lon_wins, window_cells, HEADS, head_size).astype(jnp.float32)
    grad_weights = jnp.einsum('bqhd,bkhd->bhqk', grad_heads, values)
    rounded = weights.astype(jnp.bfloat16).astype(jnp.float32)
    grad_values = jnp.einsum('bhqk,bqhd->bkhd', rounded, grad_heads)
    grad_scores = weights * (grad_weights - lax.optimization_barrier(jnp.sum(weights * grad_weights, axis=-1, keepdims=True)))
    grad_scaled = (grad_scores * head_size ** (-0.5)).astype(jnp.bfloat16).astype(jnp.float32)
    grad_queries = jnp.einsum('bhqk,bkhd->bqhd', grad_scaled, keys)
    grad_keys = jnp.einsum('bhqk,bqhd->bkhd', grad_scaled, queries)
    grad_packed = jnp.stack([grad_queries, grad_keys, grad_values], axis=2)
    grad_packed = grad_packed.reshape(lon_wins, window_cells, triple).astype(jnp.bfloat16)
    return (grad_packed, fold_bias(lax.optimization_barrier(jnp.sum(grad_scores, axis=0))))

def feed_forward(residual, grad_out, gain_vec, up_weight, down_weight):
    normed, normal_part, inv_std = layer_norm(residual, gain_vec)
    normed = normed.astype(jnp.bfloat16)
    pre_act = jnp.dot(normed, up_weight, preferred_element_type=jnp.float32)
    hidden = gelu_value(pre_act).astype(jnp.bfloat16)
    block_rows = (residual + jnp.dot(hidden, down_weight, preferred_element_type=jnp.float32)).astype(jnp.bfloat16)
    grad_wide = grad_out.astype(jnp.float32)
    grad_hidden = jnp.einsum('rc,fc->rf', grad_wide, down_weight.astype(jnp.float32))
    down_grad = jnp.einsum('rf,rc->fc', hidden.astype(jnp.float32), grad_wide)
    grad_pre = (grad_hidden * gelu_slope(pre_act)).astype(jnp.bfloat16).astype(jnp.float32)
    up_grad = jnp.einsum('rc,rf->cf', normed.astype(jnp.float32), grad_pre)
    grad_normed = jnp.einsum('rf,cf->rc', grad_pre, up_weight.astype(jnp.float32))
    grad_in, gain_grad = norm_back(grad_normed, normal_part, inv_std, gain_vec)
    return (block_rows, grad_wide + grad_in, gain_grad, up_grad, down_grad)

def lat_band(band_tokens, band_labels, band_grads, table_band, norm1_gain, qkv_weight, proj_weight, norm2_gain, up_weight, down_weight):
    lon_wins, window_cells, features = band_tokens.shape
    token_rows = band_tokens.reshape(-1, features).astype(jnp.float32)
    normed, normal_one, inv_one = layer_norm(token_rows, norm1_gain)
    normed = normed.astype(jnp.bfloat16)
    packed = jnp.dot(normed, qkv_weight, preferred_element_type=jnp.float32).astype(jnp.bfloat16)
    packed = packed.reshape(lon_wins, window_cells, 3 * features)
    mixed_heads, weights = attend(packed, table_band, band_labels)
    mixed_rows = mixed_heads.reshape(-1, features)
    branch = jnp.dot(mixed_rows, proj_weight, preferred_element_type=jnp.float32).astype(jnp.bfloat16)
    residual = token_rows + branch.astype(jnp.float32)
    block_rows, grad_resid, gain_two, up_grad, down_grad = feed_forward(residual, band_grads.reshape(-1, features), norm2_gain, up_weight, down_weight)
    branch_rows = grad_resid.astype(jnp.bfloat16).astype(jnp.float32)
    proj_grad = jnp.einsum('rc,rd->cd', mixed_rows.astype(jnp.float32), branch_rows)
    grad_mixed = jnp.einsum('rc,dc->rd', branch_rows, proj_weight.astype(jnp.float32)).astype(jnp.bfloat16)
    grad_packed, bias_part = attend_back(packed, weights, grad_mixed.reshape(lon_wins, window_cells, features))
    grad_packed = grad_packed.reshape(-1, 3 * features).astype(jnp.float32)
    qkv_grad = jnp.einsum('rc,rd->cd', normed.astype(jnp.float32), grad_packed)
    grad_normed = jnp.einsum('rc,dc->rd', grad_packed, qkv_weight.astype(jnp.float32))
    grad_shift_in, gain_one = norm_back(grad_normed, normal_one, inv_one, norm1_gain)
    grad_shift_in = grad_shift_in.astype(jnp.bfloat16)
    grad_tokens = (grad_resid + grad_shift_in.astype(jnp.float32)).astype(jnp.bfloat16)
    return (block_rows.reshape(lon_wins, window_cells, features), grad_tokens.reshape(lon_wins, window_cells, features), bias_part, (gain_one, qkv_grad, proj_grad, gain_two, up_grad, down_grad))

def reference(tokens, labels, norm1_gain, qkv_weight, proj_weight, bias_table, norm2_gain, up_weight, down_weight, cotangent):
    frame_data = jnp.roll(tokens.reshape(LEVELS, LATS, LONS, C), (-3, -6), axis=(1, 2))
    grad_frame = jnp.roll(cotangent.reshape(LEVELS, LATS, LONS, C), (-3, -6), axis=(1, 2))
    win_tokens = to_windows(frame_data)
    win_grads = to_windows(grad_frame)
    win_labels = to_windows(labels[..., None])[..., 0]
    zero_sums = (jnp.zeros((C,), jnp.float32), jnp.zeros((C, 3 * C), jnp.float32), jnp.zeros((C, C), jnp.float32), jnp.zeros((C,), jnp.float32), jnp.zeros((C, FFN), jnp.float32), jnp.zeros((FFN, C), jnp.float32))

    def band_step(carry_sums, inputs):
        band_tokens, band_labels, band_grads, table_band = inputs
        band_out, band_grad, bias_part, band_sums = lat_band(band_tokens, band_labels, band_grads, table_band, norm1_gain, qkv_weight, proj_weight, norm2_gain, up_weight, down_weight)
        return (jax.tree.map(jnp.add, carry_sums, band_sums), (band_out, band_grad, bias_part))
    totals, stacked = lax.scan(band_step, zero_sums, (win_tokens, win_labels, win_grads, bias_table))
    out_windows, grad_windows, bias_grad = stacked
    block_out = jnp.roll(from_windows(out_windows, LEVELS), (3, 6), axis=(1, 2)).reshape(LEVELS, LATS, LONS * C)
    token_grad = jnp.roll(from_windows(grad_windows, LEVELS), (3, 6), axis=(1, 2)).reshape(LEVELS, LATS, LONS * C)
    grad_scale = TOKENS ** (-0.5)
    return (block_out, token_grad, totals[0] * grad_scale, totals[1] * grad_scale, totals[2] * grad_scale, bias_grad, totals[3] * grad_scale, totals[4] * grad_scale, totals[5] * grad_scale)
```

```python
import functools

import jax
import jax.numpy as jnp
from jax import lax
from jax.experimental import pallas as pl
from jax.experimental.pallas import tpu as pltpu
from jax.sharding import PartitionSpec as P

MESH = pl.DeviceIdType.MESH
F32, BF16 = jnp.float32, jnp.bfloat16
C, HEADS, FFN = 192, 6, 768
HALF = 6 * C
EPS = 1e-05
COEFF = 0.044715
ROOT = 0.7978845608028654
MASKED = -1e30
SCALE = 32.0**-0.5
ROWS_A, ROWS_C = 2304, 1792


def nn(a, b):
    return jnp.dot(a, b, preferred_element_type=F32)


def nt(a, b):
    return lax.dot_general(a, b, (((1,), (1,)), ((), ())), preferred_element_type=F32)


def tn(a, b):
    return lax.dot_general(a, b, (((0,), (0,)), ((), ())), preferred_element_type=F32)


def mean(x):
    return jnp.sum(x, axis=-1, keepdims=True) * (1.0 / C)


def norm(x, gain):
    center = x - mean(x)
    inv = lax.rsqrt(mean(center * center) + EPS)
    xhat = center * inv
    return (xhat * gain).astype(BF16), xhat, inv


def norm_back(grad, xhat, inv, gain):
    g = grad * gain
    grad_in = inv * (g - mean(g) - xhat * mean(g * xhat))
    return grad_in, jnp.sum(grad * xhat, axis=0, keepdims=True)


def iota(shape, dim):
    return lax.broadcasted_iota(jnp.int32, shape, dim)


def cell_row(rho):
    half, r = rho >> 3, rho & 7
    level = (r * 11) >> 5
    return level * 6 + half * 3 + r - level * 3, r < 6


def flat_pieces(per, start, rows):
    at = start
    while at < start + rows:
        take = min(per - at % per, start + rows - at)
        yield at - start, at // per, at % per, take
        at += take


def kernel(
    geo, tok, lab, g1, wqkv, wproj, btab, g2, wup, wdown, cot,
    o_block, o_token, o_n1, o_qkv, o_proj, o_bias, o_n2, o_up, o_down,
    stage, ent_s, ent_r, xs, gs, labs, ytab, bias, probs, ex_s, ex_r, rows_st,
    buf_a, buf_c, r1a, r1c, m1a, m1c, r2a, r2c, acc2, r3, z4, fin, nst,
    zfold, ffold, bst, b_s, b_r1, b_y, b_fin,
    *sems,
):
    nlat, nlon, ny_lo, nx, nz, ny_hi = geo
    ny = ny_lo * ny_hi
    pieces = 2 * nx
    ra, rc = ROWS_A // pieces, ROWS_C // pieces
    ry = (ra + rc) // ny
    cells = 144 * nlat * nlon
    (s_ent, s_exb, s_ext, s_1a, s_1c, s_2a, s_2c, s_3, s_4, s_5, s_6, s_7, s_b1, s_b2, s_b3) = [
        (sems[2 * i], sems[2 * i + 1]) for i in range(15)
    ]

    lat, lon = lax.axis_index("lat"), lax.axis_index("lon")
    core = lax.rem(lat, 2)
    x = lax.rem(lat // 2, nx)
    y_lo = lat // (2 * nx)
    z = lon // ny_hi
    y_hi = lax.rem(lon, ny_hi)
    y = y_hi * ny_lo + y_lo

    def at_core():
        return (lat + 1 - 2 * core, lon)

    def at_x(k):
        return ((y_lo * nx + lax.rem(x + k, nx)) * 2 + core, lon)

    def at_y(k):
        other = lax.rem(y + k, ny)
        return ((lax.rem(other, ny_lo) * nx + x) * 2 + core, z * ny_hi + other // ny_lo)

    def at_yhi(k):
        return (lat, z * ny_hi + lax.rem(y_hi + k, ny_hi))

    def at_z(k):
        return (lat, lax.rem(z + k, nz) * ny_hi + y_hi)

    def near(da, db):
        return (lax.rem(lat + da + nlat, nlat), lax.rem(lon + db + nlon, nlon))

    def push(src, dst, sem, i, dev):
        copy = pltpu.make_async_remote_copy(
            src_ref=src, dst_ref=dst, send_sem=sem[0].at[i], recv_sem=sem[1].at[i],
            device_id=dev, device_id_type=MESH,
        )
        copy.start()
        return copy

    barrier = pltpu.get_barrier_semaphore()
    partners = [at_core()]
    partners += [at_x(k) for k in range(1, nx)]
    partners += [at_y(k) for k in range(1, ny)]
    partners += [at_z(k) for k in range(1, nz)]
    partners += [near(-1, 0), near(0, -1), near(-1, -1), near(1, 0), near(0, 1), near(1, 1)]
    for dev in partners:
        pl.semaphore_signal(barrier, inc=1, device_id=dev, device_id_type=MESH)

    stage[...] = jnp.zeros_like(stage)
    for half in range(2):
        for part in range(2):
            for kind, ref in enumerate((tok, cot)):
                for level in range(2):
                    rows = ref[level].astype(F32)
                    stage[half * 2 + part, pl.ds(kind * 8 + level * 3, 3), :] = rows[
                        half * 3 : half * 3 + 3, part * HALF : (part + 1) * HALF
                    ]
    for i in range(3):
        ent_s[i] = stage[i].astype(BF16)
    pl.semaphore_wait(barrier, len(partners))
    entry = [
        push(ent_s.at[i], ent_r.at[i], s_ent, i, near(half - 1, part - 1))
        for i, (half, part) in enumerate(((0, 0), (0, 1), (1, 0)))
    ]

    labs[...] = jnp.full_like(labs, -1.0)
    for half in range(2):
        for level in range(2):
            labs[pl.ds(half * 8 + level * 3, 3), pl.ds(0, 12)] = lab[
                level, half * 3 : half * 3 + 3, :
            ].astype(F32)
    lab16 = labs[...].astype(BF16)
    pick = (11 - (iota((192, 128), 0) >> 4) == iota((192, 128), 1)).astype(F32).astype(BF16)
    lane_all = nt(lab16, pick)
    lane_lab = jnp.sum(
        jnp.where(iota((16, 192), 0) == (iota((16, 192), 1) & 15), lane_all, 0.0),
        axis=0, keepdims=True,
    )
    row_all = nt(pick, lab16)
    row_lab = jnp.sum(
        jnp.where(iota((192, 16), 1) == (iota((192, 16), 0) & 15), row_all, 0.0),
        axis=1, keepdims=True,
    )
    same = row_lab == lane_lab

    place, real = cell_row(iota((16, 144), 0))
    spot = iota((16, 144), 1)
    spot_row = (spot * 171) >> 11
    m1 = jnp.where((spot_row == place) & real, 1.0, 0.0)
    place_j, real_j = cell_row(iota((144, 192), 1) & 15)
    spot_j = iota((144, 192), 0)
    spot_col = spot_j - ((spot_j * 171) >> 11) * 12
    m2 = jnp.where((spot_col == place_j) & real_j, 1.0, 0.0).astype(BF16)
    group = iota((192, 192), 1) >> 4

    def build(h, carry):
        table = btab[0, h]
        left = table
        full = jnp.zeros((368, 192), F32)
        for _ in range(3):
            piece = left.astype(BF16).astype(F32)
            left = left - piece
            wide = (piece[:, None, :] * m1[None]).reshape(368, 144)
            full = full + nn(wide.astype(BF16), m2)
        ytab[...] = full
        out = ytab[pl.ds(176, 192), :]
        for bj in range(1, 12):
            out = jnp.where(group == bj, ytab[pl.ds((11 - bj) * 16, 192), :], out)
        bias[h] = jnp.where(same, out, MASKED)
        return carry

    lax.fori_loop(0, HEADS, build, 0)
    buf_c[...] = jnp.zeros_like(buf_c)
    nst[...] = jnp.zeros_like(nst)
    bst[...] = jnp.zeros_like(bst)

    def lay(quarter, half, part):
        for c in range(6):
            row = (11 - part * 6 - c) * 16 + half * 8
            xs[pl.ds(row, 8), :] = quarter[0:8, c * C : (c + 1) * C]
            gs[pl.ds(row, 8), :] = quarter[8:16, c * C : (c + 1) * C]

    lay(stage[3], 0, 0)
    for i, (half, part) in enumerate(((1, 1), (1, 0), (0, 1))):
        entry[i].wait()
        lay(ent_r[i].astype(F32), half, part)

    gain1, gain2 = g1[...], g2[...]
    tokens = xs[...]
    n1, xhat1, inv1 = norm(tokens, gain1)
    packed = nn(n1, wqkv[...]).astype(BF16)
    q, k, v = packed[:, :C], packed[:, C : 2 * C], packed[:, 2 * C :]
    head_of = iota((1, C), 1) >> 5
    masks = [(head_of == h).astype(F32).astype(BF16) for h in range(HEADS)]
    mixed = jnp.zeros((192, C), F32)
    for h in range(HEADS):
        s = nt(q * masks[h], k) * SCALE + bias[h]
        e = jnp.exp(s - jnp.max(s, axis=-1, keepdims=True))
        p = e * (1.0 / jnp.sum(e, axis=-1, keepdims=True))
        probs[h] = p
        mixed = mixed + nn(p.astype(BF16), v * masks[h])
    mixed = mixed.astype(BF16)
    branch = nn(mixed, wproj[...]).astype(BF16)
    residual = tokens + branch.astype(F32)
    n2, xhat2, inv2 = norm(residual, gain2)
    pre = nn(n2, wup[...])
    square = pre * pre
    tanh = jnp.tanh(ROOT * (pre + COEFF * pre * square))
    hidden = (0.5 * pre * (1.0 + tanh)).astype(BF16)
    slope = 0.5 * (1.0 + tanh) + 0.5 * pre * (1.0 - tanh * tanh) * ROOT * (
        1.0 + 3.0 * COEFF * square
    )
    block = residual + nn(hidden, wdown[...])

    def leave(which, value, sem):
        rows_st[...] = value
        copies = []
        for half in range(2):
            for part in range(2):
                i = half * 2 + part
                out = ex_r.at[which, 0] if i == 0 else ex_s.at[which, i]
                for c in range(6):
                    row = (11 - part * 6 - c) * 16 + half * 8
                    out[:, pl.ds(c * C, C)] = rows_st[pl.ds(row, 8), :]
                if i:
                    copies.append(
                        push(ex_s.at[which, i], ex_r.at[which, i], sem, i - 1, near(half, part))
                    )
        return copies

    exit_block = leave(0, block, s_exb)

    grads = gs[...]
    grads16 = grads.astype(BF16)
    grad_pre = (nt(grads16, wdown[...]) * slope).astype(BF16)
    down = tn(hidden, grads16)
    up = tn(n2, grad_pre)

    def put(buf, per, start, value, lanes=(0, 128)):
        value = value.astype(BF16)
        for src, piece, row, take in flat_pieces(per, start, value.shape[0]):
            buf[piece, pl.ds(row, take), pl.ds(lanes[0], lanes[1] - lanes[0])] = value[
                src : src + take
            ]

    for i in range(6):
        put(buf_a, ra, i * 192, up[:, i * 128 : (i + 1) * 128])
    put(buf_a, ra, 1152, down[:, :128])
    put(buf_a, ra, 1920, down[:384, 128:], (0, 64))
    put(buf_a, ra, 1920, down[384:, 128:], (64, 128))
    other = pl.ds((1 - core) * nx, nx)
    copy_1a = push(buf_a.at[other], r1a, s_1a, 0, at_core())

    grad_n2 = nt(grad_pre, wup[...])
    grad_in, norm2 = norm_back(grad_n2, xhat2, inv2, gain2)
    grad_res = grads + grad_in
    grad_branch = grad_res.astype(BF16)
    proj = tn(mixed, grad_branch)
    grad_mixed = nt(grad_branch, wproj[...]).astype(BF16)

    dq = jnp.zeros((192, C), F32)
    dk = jnp.zeros((192, C), F32)
    dv = jnp.zeros((192, C), F32)
    copies_2a = []
    for h in range(HEADS):
        gm = grad_mixed * masks[h]
        p = probs[h]
        dp = nt(gm, v)
        t = p * dp
        ds = ((t - p * jnp.sum(t, axis=-1, keepdims=True)) * SCALE).astype(BF16)
        zfold[h] = ds
        dv = dv + tn(p.astype(BF16), gm)
        dk = dk + tn(ds, q * masks[h])
        dq = dq + nn(ds, k * masks[h])
        if h == 1:
            copy_1a.wait()
            for i in range(nx):
                m1a[i] = (buf_a[core * nx + i].astype(F32) + r1a[i].astype(F32)).astype(BF16)
            copies_2a = [
                push(m1a.at[lax.rem(x + j, nx)], r2a.at[j - 1], s_2a, j - 1, at_x(j))
                for j in range(1, nx)
            ]
    grad_packed = jnp.concatenate([dq, dk, dv], axis=1).astype(BF16)
    qkv = tn(n1, grad_packed)
    grad_n1 = nt(grad_packed, wqkv[...])
    grad_in1, norm1 = norm_back(grad_n1, xhat1, inv1, gain1)

    for i in range(4):
        put(buf_c, rc, i * 192, qkv[:, i * 128 : (i + 1) * 128])
    put(buf_c, rc, 768, proj[:, :128])
    put(buf_c, rc, 960, qkv[:, 512:], (0, 64))
    put(buf_c, rc, 960, proj[:, 128:], (64, 128))
    nst[0:1, :] = norm1[:, :128]
    nst[1:2, 0:64] = norm1[:, 128:]
    nst[2:3, :] = norm2[:, :128]
    nst[3:4, 0:64] = norm2[:, 128:]
    put(buf_c, rc, 1152, nst[...])
    copy_1c = push(buf_c.at[other], r1c, s_1c, 0, at_core())

    token_grad = grad_res + grad_in1.astype(BF16).astype(F32)
    exit_token = leave(1, token_grad, s_ext)

    copy_1c.wait()
    for i in range(nx):
        m1c[i] = (buf_c[core * nx + i].astype(F32) + r1c[i].astype(F32)).astype(BF16)
    copies_2c = [
        push(m1c.at[lax.rem(x + j, nx)], r2c.at[j - 1], s_2c, j - 1, at_x(j)) for j in range(1, nx)
    ]

    def fold(h, carry):
        ds = zfold[h]
        ffold[...] = jnp.zeros_like(ffold)
        for bj in range(12):
            one = (iota((1, 192), 1) >> 4 == bj).astype(F32).astype(BF16)
            ffold[pl.ds((11 - bj) * 16, 192), :] += ds * one
        wide = nt(ffold[...], m2).reshape(23, 16, 144) * m1[None]
        o_bias[0, h] = jnp.sum(wide, axis=1) * (1.0 / SCALE)
        return carry

    lax.fori_loop(0, HEADS, fold, 0)
    for h in range(HEADS):
        bst[pl.ds(h * 24, 23), :] = o_bias[0, h, :, 0:128]
        bst[pl.ds(144, 23), pl.ds(h * 16, 16)] = o_bias[0, h, :, 128:144]
    rb = 256 // nz
    b_s[...] = bst[...].astype(BF16).reshape(nz, rb, 128)
    copies_b1 = [
        push(b_s.at[lax.rem(z + j, nz)], b_r1.at[j - 1], s_b1, j - 1, at_z(j)) for j in range(1, nz)
    ]

    def gather_sum(own, copies, slots):
        total = own.astype(F32)
        for i, copy in enumerate(copies):
            copy.wait()
            total = total + slots[i].astype(F32)
        return total.astype(BF16)

    own_a = m1a[x]
    acc2[pl.ds(0, ra), :] = gather_sum(own_a, copies_2a, r2a)
    acc2[pl.ds(ra, rc), :] = gather_sum(m1c[x], copies_2c, r2c)

    def part_y(ref, index):
        return ref.at[pl.ds(pl.multiple_of(index * ry, 16), ry)]

    copies_3 = [
        push(part_y(acc2, lax.rem(y + j, ny)), r3.at[j - 1], s_3, j - 1, at_y(j))
        for j in range(1, ny)
    ]

    b_y[y_hi] = gather_sum(b_s[z], copies_b1, b_r1)
    copies_b2 = [
        push(b_y.at[y_hi], b_y.at[y_hi], s_b2, j - 1, at_yhi(j)) for j in range(1, ny_hi)
    ]

    z4[z] = gather_sum(part_y(acc2, y)[...], copies_3, r3)
    copies_4 = [push(z4.at[z], z4.at[z], s_4, j - 1, at_z(j)) for j in range(1, nz)]

    for copy in copies_b2:
        copy.wait()
    total = b_y[0].astype(F32)
    for i in range(1, ny_hi):
        total = total + b_y[i].astype(F32)
    b_fin[z] = total.astype(BF16)
    copies_b3 = [push(b_fin.at[z], b_fin.at[z], s_b3, j - 1, at_z(j)) for j in range(1, nz)]

    for copy in copies_4:
        copy.wait()
    total = z4[0].astype(F32)
    for i in range(1, nz):
        total = total + z4[i].astype(F32)
    mine = core * nx + x
    done = part_y(fin.at[mine], y)
    done[...] = total.astype(BF16)
    copies_5 = [push(done, done, s_5, j - 1, at_y(j)) for j in range(1, ny)]

    def arrive(which, copies, out):
        for copy in copies:
            copy.wait()
        for half in range(2):
            for part in range(2):
                i = (1 - half) * 2 + 1 - part
                for level in range(2):
                    out[level, pl.ds(half * 3, 3), pl.ds(part * HALF, HALF)] = ex_r[
                        which, i, pl.ds(level * 3, 3), :
                    ].astype(BF16)

    arrive(0, exit_block, o_block)
    arrive(1, exit_token, o_token)

    for copy in copies_5:
        copy.wait()
    copies_6 = [push(fin.at[mine], fin.at[mine], s_6, j - 1, at_x(j)) for j in range(1, nx)]
    for copy in copies_b3:
        copy.wait()
    flat = b_fin[...].reshape(256, 128).astype(F32)
    for h in range(HEADS):
        o_bias[0, h, :, 0:128] = flat[h * 24 : h * 24 + 23]
        o_bias[0, h, :, 128:144] = flat[144:167, h * 16 : h * 16 + 16]
    for copy in copies_6:
        copy.wait()
    ours = fin.at[pl.ds(core * nx, nx)]
    push(ours, ours, s_7, 0, at_core()).wait()

    scale = float(cells) ** (-0.5)

    def take(per, base, start, rows):
        parts = [
            fin[piece, pl.ds(base + row, count), :]
            for _, piece, row, count in flat_pieces(per, start, rows)
        ]
        whole = parts[0] if len(parts) == 1 else jnp.concatenate(parts, axis=0)
        return whole.astype(F32) * scale

    for i in range(6):
        o_up[:, pl.ds(i * 128, 128)] = take(ra, 0, i * 192, 192)
    o_down[:, 0:128] = take(ra, 0, 1152, 768)
    rest = take(ra, 0, 1920, 384)
    o_down[0:384, 128:192] = rest[:, :64]
    o_down[384:768, 128:192] = rest[:, 64:]
    for i in range(4):
        o_qkv[:, pl.ds(i * 128, 128)] = take(rc, ra, i * 192, 192)
    o_proj[:, 0:128] = take(rc, ra, 768, 192)
    rest = take(rc, ra, 960, 192)
    o_qkv[:, 512:576] = rest[:, :64]
    o_proj[:, 128:192] = rest[:, 64:]
    rest = take(rc, ra, 1152, 16)
    o_n1[:, 0:128] = rest[0:1, :]
    o_n1[:, 128:192] = rest[1:2, :64]
    o_n2[:, 0:128] = rest[2:3, :]
    o_n2[:, 128:192] = rest[3:4, :64]


def on_device(geo, tokens, labels, gain1, wqkv, wproj, table, gain2, wup, wdown, cotangent):
    nlat, nlon, ny_lo, nx, nz, ny_hi = geo
    ny = ny_lo * ny_hi
    pieces = 2 * nx
    ra, rc = ROWS_A // pieces, ROWS_C // pieces
    ry = (ra + rc) // ny
    rb = 256 // nz
    vmem = pltpu.VMEM
    scratch = [
        vmem((4, 16, HALF), F32),
        vmem((3, 16, HALF), BF16),
        vmem((3, 16, HALF), BF16),
        vmem((192, C), F32),
        vmem((192, C), F32),
        vmem((16, 128), F32),
        vmem((368, 192), F32),
        vmem((HEADS, 192, 192), F32),
        vmem((HEADS, 192, 192), F32),
        vmem((2, 4, 8, HALF), F32),
        vmem((2, 4, 8, HALF), F32),
        vmem((192, C), F32),
        vmem((pieces, ra, 128), BF16),
        vmem((pieces, rc, 128), BF16),
        vmem((nx, ra, 128), BF16),
        vmem((nx, rc, 128), BF16),
        vmem((nx, ra, 128), BF16),
        vmem((nx, rc, 128), BF16),
        vmem((nx - 1, ra, 128), BF16),
        vmem((nx - 1, rc, 128), BF16),
        vmem((ra + rc, 128), BF16),
        vmem((ny - 1, ry, 128), BF16),
        vmem((nz, ry, 128), BF16),
        vmem((pieces, ra + rc, 128), BF16),
        vmem((16, 128), F32),
        vmem((HEADS, 192, 192), BF16),
        vmem((368, 192), BF16),
        vmem((256, 128), F32),
        vmem((nz, rb, 128), BF16),
        vmem((nz - 1, rb, 128), BF16),
        vmem((ny_hi, rb, 128), BF16),
        vmem((nz, rb, 128), BF16),
    ]
    for count in (3, 3, 3, 1, 1, nx - 1, nx - 1, ny - 1, nz - 1, ny - 1, nx - 1, 1, nz - 1, ny_hi - 1, nz - 1):
        scratch += [pltpu.SemaphoreType.DMA((count,)), pltpu.SemaphoreType.DMA((count,))]
    shape = jax.ShapeDtypeStruct
    whole = pl.BlockSpec(memory_space=vmem)
    out = pl.pallas_call(
        functools.partial(kernel, geo),
        out_shape=(
            shape(tokens.shape, BF16),
            shape(tokens.shape, BF16),
            shape((1, C), F32),
            shape((C, 3 * C), F32),
            shape((C, C), F32),
            shape(table.shape, F32),
            shape((1, C), F32),
            shape((C, FFN), F32),
            shape((FFN, C), F32),
        ),
        in_specs=[whole] * 10,
        out_specs=(whole,) * 9,
        scratch_shapes=scratch,
        compiler_params=pltpu.CompilerParams(
            collective_id=0, has_side_effects=True, vmem_limit_bytes=48 * 1024 * 1024
        ),
    )(
        tokens, labels, gain1.reshape(1, C), wqkv, wproj, table, gain2.reshape(1, C), wup, wdown,
        cotangent,
    )
    out = list(out)
    out[2] = out[2].reshape(C)
    out[6] = out[6].reshape(C)
    return tuple(out)


def geometry(mesh):
    nlat, nlon = mesh.shape["lat"], mesh.shape["lon"]
    ny_hi = 4 if nlon == 32 else 2
    nx = min(4, nlat // 2)
    return nlat, nlon, nlat // 2 // nx, nx, nlon // ny_hi, ny_hi


def solution(mesh):
    cells, band = P(None, "lat", "lon"), P("lat", None, None, None)
    return jax.shard_map(
        functools.partial(on_device, geometry(mesh)),
        mesh=mesh,
        in_specs=(cells, cells, P(), P(), P(), band, P(), P(), P(), cells),
        out_specs=(cells, cells, P(), P(), P(), band, P(), P(), P()),
        check_vma=False,
    )
```

```python
import functools

import jax
import jax.numpy as jnp
from jax import lax
from jax.experimental import pallas as pl
from jax.experimental.pallas import tpu as pltpu
from jax.sharding import PartitionSpec as P

MESH = pl.DeviceIdType.MESH
F32, BF16 = jnp.float32, jnp.bfloat16
C, HEADS, FFN = 192, 6, 768
HALF = 6 * C
EPS = 1e-05
COEFF = 0.044715
ROOT = 0.7978845608028654
MASKED = -1e30
SCALE = 32.0**-0.5
ROWS = (2048, 768, 768)


def nn(a, b):
    return jnp.dot(a, b, preferred_element_type=F32)


def nt(a, b):
    return lax.dot_general(a, b, (((1,), (1,)), ((), ())), preferred_element_type=F32)


def tn(a, b):
    return lax.dot_general(a, b, (((0,), (0,)), ((), ())), preferred_element_type=F32)


def mean(x):
    return jnp.sum(x, axis=-1, keepdims=True) * (1.0 / C)


def norm(x, gain):
    center = x - mean(x)
    inv = lax.rsqrt(mean(center * center) + EPS)
    xhat = center * inv
    return (xhat * gain).astype(BF16), xhat, inv


def norm_back(grad, xhat, inv, gain):
    g = grad * gain
    grad_in = inv * (g - mean(g) - xhat * mean(g * xhat))
    return grad_in, jnp.sum(grad * xhat, axis=0, keepdims=True)


def iota(shape, dim):
    return lax.broadcasted_iota(jnp.int32, shape, dim)


def cell_row(rho):
    half, r = rho >> 3, rho & 7
    return (r & 1) * 6 + half * 3 + (r >> 1), r < 6


def flat_pieces(sizes, start, rows):
    at = start
    while at < start + rows:
        group, base = 0, 0
        while at >= base + ROWS[group]:
            base += ROWS[group]
            group += 1
        per = sizes[group]
        inside = at - base
        take = min(per - inside % per, start + rows - at)
        yield at - start, group, inside // per, inside % per, take
        at += take


def kernel(
    geo, *refs,
):
    inputs, outs, held, ready, refs = refs[:10], refs[10:19], refs[19:29], refs[29:38], refs[38:]
    tok, lab, g1, wqkv, wproj, btab, g2, wup, wdown, cot = held
    o_block, o_token, o_n1, o_qkv, o_proj, o_bias, o_n2, o_up, o_down = ready
    (
        stage, ent_s, ent_r, xs, gs, labs, ytab, bias, probs, ex_s, ex_r, rows_st,
        nst, zfold, ffold, fsum, bst, b_s, b_r1, b_y, b_fin,
        buf_a, c_a, m1_a, r2_a, m2_a, r3_a, z_a, fin_a,
        buf_b, c_b, m1_b, r2_b, x_b, z_b, fin_b,
        buf_d, c_d, m1_d, r2_d, x_d, z_d, fin_d,
    ) = refs[:43]
    in_sem, out_sem, *sems = refs[43:]
    loads = {}
    for i in (0, 9, 1, 5, 2, 3, 4, 6, 7, 8):
        loads[i] = pltpu.make_async_copy(inputs[i], held[i], in_sem.at[i])
        loads[i].start()
    nlat, nlon, ny_lo, nx, nz, ny_hi = geo
    ny = ny_lo * ny_hi
    per = piece_rows(geo)
    bufs, fins = (buf_a, buf_b, buf_d), (fin_a, fin_b, fin_d)
    cells = 144 * nlat * nlon
    s_ent, s_exb, s_ext, s_b1, s_b2, s_b3, *s_groups = [
        (sems[2 * i], sems[2 * i + 1]) for i in range(len(sems) // 2)
    ]
    s_a, s_b, s_d = s_groups[:7], s_groups[7:13], s_groups[13:19]

    lat, lon = lax.axis_index("lat"), lax.axis_index("lon")
    core = lax.rem(lat, 2)
    x = lax.rem(lat // 2, nx)
    y_lo = lat // (2 * nx)
    z = lon // ny_hi
    y_hi = lax.rem(lon, ny_hi)
    y = y_hi * ny_lo + y_lo

    def at_core():
        return (lat + 1 - 2 * core, lon)

    def at_x(k):
        return ((y_lo * nx + lax.rem(x + k, nx)) * 2 + core, lon)

    def at_y(k):
        other = lax.rem(y + k, ny)
        return ((lax.rem(other, ny_lo) * nx + x) * 2 + core, z * ny_hi + other // ny_lo)

    def at_yhi(k):
        return (lat, z * ny_hi + lax.rem(y_hi + k, ny_hi))

    def at_z(k):
        return (lat, lax.rem(z + k, nz) * ny_hi + y_hi)

    def near(da, db):
        return (lax.rem(lat + da + nlat, nlat), lax.rem(lon + db + nlon, nlon))

    def push(src, dst, sem, i, dev):
        copy = pltpu.make_async_remote_copy(
            src_ref=src, dst_ref=dst, send_sem=sem[0].at[i], recv_sem=sem[1].at[i],
            device_id=dev, device_id_type=MESH,
        )
        copy.start()
        return copy

    barrier = pltpu.get_barrier_semaphore()
    partners = [at_core()]
    partners += [at_x(k) for k in range(1, nx)]
    partners += [at_y(k) for k in range(1, ny)]
    partners += [at_z(k) for k in range(1, nz)]
    partners += [near(-1, 0), near(0, -1), near(-1, -1), near(1, 0), near(0, 1), near(1, 1)]
    for dev in partners:
        pl.semaphore_signal(barrier, inc=1, device_id=dev, device_id_type=MESH)

    loads[0].wait()
    loads[9].wait()

    stage[...] = jnp.zeros_like(stage)
    for half in range(2):
        for part in range(2):
            for kind, ref in enumerate((tok, cot)):
                for row in range(3):
                    stage[half * 2 + part, pl.ds(kind * 8 + row * 2, 2), :] = ref[
                        half * 3 + row, :, pl.ds(part * HALF, HALF)
                    ].astype(F32)
    for i in range(3):
        ent_s[i] = stage[i].astype(BF16)
    pl.semaphore_wait(barrier, len(partners))
    entry = [
        push(ent_s.at[i], ent_r.at[i], s_ent, i, near(half - 1, part - 1))
        for i, (half, part) in enumerate(((0, 0), (0, 1), (1, 0)))
    ]

    loads[1].wait()
    loads[5].wait()

    labs[...] = jnp.full_like(labs, -1.0)
    for half in range(2):
        for row in range(3):
            labs[pl.ds(half * 8 + row * 2, 2), pl.ds(0, 12)] = lab[half * 3 + row].astype(F32)
    lab16 = labs[...].astype(BF16)
    pick = (11 - (iota((192, 128), 0) >> 4) == iota((192, 128), 1)).astype(F32).astype(BF16)
    lane_all = nt(lab16, pick)
    lane_lab = jnp.sum(
        jnp.where(iota((16, 192), 0) == (iota((16, 192), 1) & 15), lane_all, 0.0),
        axis=0, keepdims=True,
    )
    row_all = nt(pick, lab16)
    row_lab = jnp.sum(
        jnp.where(iota((192, 16), 1) == (iota((192, 16), 0) & 15), row_all, 0.0),
        axis=1, keepdims=True,
    )
    same = row_lab == lane_lab

    place, real = cell_row(iota((16, 144), 0))
    spot = iota((16, 144), 1)
    spot_row = (spot * 171) >> 11
    m1 = jnp.where((spot_row == place) & real, 1.0, 0.0)
    place_j, real_j = cell_row(iota((144, 192), 1) & 15)
    spot_j = iota((144, 192), 0)
    spot_col = spot_j - ((spot_j * 171) >> 11) * 12
    m2 = jnp.where((spot_col == place_j) & real_j, 1.0, 0.0).astype(BF16)
    group = iota((192, 192), 1) >> 4

    def build(h, carry):
        left = btab[h]
        full = jnp.zeros((368, 192), F32)
        for _ in range(3):
            piece = left.astype(BF16).astype(F32)
            left = left - piece
            wide = (piece * m1[None]).reshape(368, 144)
            full = full + nn(wide.astype(BF16), m2)
        ytab[...] = full
        out = ytab[pl.ds(176, 192), :]
        for bj in range(1, 12):
            out = jnp.where(group == bj, ytab[pl.ds((11 - bj) * 16, 192), :], out)
        bias[h] = jnp.where(same, out, MASKED)
        return carry

    lax.fori_loop(0, HEADS, build, 0)
    buf_d[...] = jnp.zeros_like(buf_d)
    nst[...] = jnp.zeros_like(nst)
    bst[...] = jnp.zeros_like(bst)

    def lay(quarter, half, part):
        for c in range(6):
            row = (11 - part * 6 - c) * 16 + half * 8
            xs[pl.ds(row, 8), :] = quarter[0:8, c * C : (c + 1) * C]
            gs[pl.ds(row, 8), :] = quarter[8:16, c * C : (c + 1) * C]

    for i in (2, 3, 4, 6, 7, 8):
        loads[i].wait()
    lay(stage[3], 0, 0)
    for i, (half, part) in enumerate(((1, 1), (1, 0), (0, 1))):
        entry[i].wait()
        lay(ent_r[i].astype(F32), half, part)

    gain1, gain2 = g1[...], g2[...]
    tokens = xs[...]
    n1, xhat1, inv1 = norm(tokens, gain1)
    packed = nn(n1, wqkv[...]).astype(BF16)
    q, k, v = packed[:, :C], packed[:, C : 2 * C], packed[:, 2 * C :]
    head_of = iota((1, C), 1) >> 5
    masks = [(head_of == h).astype(F32).astype(BF16) for h in range(HEADS)]
    mixed = jnp.zeros((192, C), F32)
    for h in range(HEADS):
        s = nt(q * masks[h], k) * SCALE + bias[h]
        e = jnp.exp(s - jnp.max(s, axis=-1, keepdims=True))
        p = e * (1.0 / jnp.sum(e, axis=-1, keepdims=True))
        probs[h] = p
        mixed = mixed + nn(p.astype(BF16), v * masks[h])
    mixed = mixed.astype(BF16)
    branch = nn(mixed, wproj[...]).astype(BF16)
    residual = tokens + branch.astype(F32)
    n2, xhat2, inv2 = norm(residual, gain2)
    pre = nn(n2, wup[...])
    square = pre * pre
    tanh = jnp.tanh(ROOT * (pre + COEFF * pre * square))
    hidden = (0.5 * pre * (1.0 + tanh)).astype(BF16)
    slope = 0.5 * (1.0 + tanh) + 0.5 * pre * (1.0 - tanh * tanh) * ROOT * (
        1.0 + 3.0 * COEFF * square
    )
    block = residual + nt(hidden, wdown[...])

    def leave(which, value, sem):
        rows_st[...] = value
        copies = []
        for half in range(2):
            for part in range(2):
                i = half * 2 + part
                out = ex_r.at[which, 0] if i == 0 else ex_s.at[which, i]
                for c in range(6):
                    row = (11 - part * 6 - c) * 16 + half * 8
                    out[:, pl.ds(c * C, C)] = rows_st[pl.ds(row, 8), :]
                if i:
                    copies.append(
                        push(ex_s.at[which, i], ex_r.at[which, i], sem, i - 1, near(half, part))
                    )
        return copies

    exit_block = leave(0, block, s_exb)

    grads = gs[...]
    grads16 = grads.astype(BF16)
    grad_pre = (nn(grads16, wdown[...]) * slope).astype(BF16)
    down = tn(grads16, hidden)
    up = tn(n2, grad_pre)

    def put(start, value, lanes=(0, 128)):
        value = value.astype(BF16)
        for src, group, piece, row, take in flat_pieces(per, start, value.shape[0]):
            bufs[group][piece, pl.ds(row, take), pl.ds(lanes[0], lanes[1] - lanes[0])] = value[
                src : src + take
            ]

    for i in range(6):
        put(i * 192, up[:, i * 128 : (i + 1) * 128])
        put(1152 + i * 192, down[:, i * 128 : (i + 1) * 128])

    def half_to_core(buf, dst, sem, count):
        return push(buf.at[pl.ds((1 - core) * count, count)], dst, sem, 0, at_core())

    def own_half(buf, other, out, count, copy):
        copy.wait()
        for i in range(count):
            out[i] = (buf[core * count + i].astype(F32) + other[i].astype(F32)).astype(BF16)

    def deal(pieces, slots, sem, me, count, where):
        return [
            push(pieces(lax.rem(me + j, count)), slots.at[j - 1], sem, j - 1, where(j))
            for j in range(1, count)
        ]

    def share(ref, sem, count, where):
        return [push(ref, ref, sem, j - 1, where(j)) for j in range(1, count)]

    def sum_dealt(own, copies, slots):
        total = own.astype(F32)
        for i, copy in enumerate(copies):
            copy.wait()
            total = total + slots[i].astype(F32)
        return total.astype(BF16)

    def sum_shared(copies, slots, count):
        for copy in copies:
            copy.wait()
        total = slots[0].astype(F32)
        for i in range(1, count):
            total = total + slots[i].astype(F32)
        return total.astype(BF16)

    copies_a = half_to_core(buf_a, c_a, s_a[0], nx)

    grad_n2 = nt(grad_pre, wup[...])
    grad_in, norm2 = norm_back(grad_n2, xhat2, inv2, gain2)
    grad_res = grads + grad_in
    grad_branch = grad_res.astype(BF16)
    proj = tn(mixed, grad_branch)
    grad_mixed = nt(grad_branch, wproj[...]).astype(BF16)

    def piece_of(ref, index):
        size = per[0] // ny
        return ref.at[pl.ds(pl.multiple_of(index * size, 16), size)]

    dq = jnp.zeros((192, C), F32)
    dk = jnp.zeros((192, C), F32)
    dv = jnp.zeros((192, C), F32)
    for h in range(HEADS):
        gm = grad_mixed * masks[h]
        p = probs[h]
        dp = nt(gm, v)
        t = p * dp
        ds = ((t - p * jnp.sum(t, axis=-1, keepdims=True)) * SCALE).astype(BF16)
        zfold[h] = ds
        dv = dv + tn(p.astype(BF16), gm)
        dk = dk + tn(ds, q * masks[h])
        dq = dq + nn(ds, k * masks[h])
        if h == 1:
            own_half(buf_a, c_a, m1_a, nx, copies_a)
            copies_a = deal(lambda i: m1_a.at[i], r2_a, s_a[1], x, nx, at_x)
        if h == 5:
            m2_a[...] = sum_dealt(m1_a[x], copies_a, r2_a)
            copies_a = deal(lambda i: piece_of(m2_a, i), r3_a, s_a[2], y, ny, at_y)
    grad_packed = jnp.concatenate([dq, dk, dv], axis=1).astype(BF16)
    qkv = tn(n1, grad_packed)
    grad_n1 = nt(grad_packed, wqkv[...])
    grad_in1, norm1 = norm_back(grad_n1, xhat1, inv1, gain1)

    for i in range(4):
        put(2304 + i * 192, qkv[:, i * 128 : (i + 1) * 128])
    put(3072, proj[:, :128])
    put(3264, qkv[:, 512:], (0, 64))
    put(3264, proj[:, 128:], (64, 128))
    nst[0:1, :] = norm1[:, :128]
    nst[1:2, 0:64] = norm1[:, 128:]
    nst[2:3, :] = norm2[:, :128]
    nst[3:4, 0:64] = norm2[:, 128:]
    put(3456, nst[...])
    copies_b = half_to_core(buf_b, c_b, s_b[0], ny)
    copies_d = half_to_core(buf_d, c_d, s_d[0], nz)

    token_grad = grad_res + grad_in1.astype(BF16).astype(F32)
    exit_token = leave(1, token_grad, s_ext)

    z_a[z] = sum_dealt(piece_of(m2_a, y)[...], copies_a, r3_a)
    copies_a = share(z_a.at[z], s_a[3], nz, at_z)
    own_half(buf_b, c_b, m1_b, ny, copies_b)
    copies_b = deal(lambda i: m1_b.at[i], r2_b, s_b[1], y, ny, at_y)
    own_half(buf_d, c_d, m1_d, nz, copies_d)
    copies_d = deal(lambda i: m1_d.at[i], r2_d, s_d[1], z, nz, at_z)

    def fold(h, carry):
        ds = zfold[h]
        ffold[...] = jnp.zeros_like(ffold)
        for bj in range(12):
            one = (iota((1, 192), 1) >> 4 == bj).astype(F32).astype(BF16)
            ffold[pl.ds((11 - bj) * 16, 192), :] += ds * one
        wide = nt(ffold[...], m2).reshape(23, 16, 144) * m1[None]
        fsum[h, 0:23, :] = jnp.sum(wide, axis=1) * (1.0 / SCALE)
        return carry

    lax.fori_loop(0, HEADS, fold, 0)
    for h in range(HEADS):
        bst[pl.ds(h * 24, 23), :] = fsum[h, 0:23, 0:128]
        bst[pl.ds(144, 23), pl.ds(h * 16, 16)] = fsum[h, 0:23, 128:144]
    rb = 256 // nz
    b_s[...] = bst[...].astype(BF16).reshape(nz, rb, 128)
    copies_bias = deal(lambda i: b_s.at[i], b_r1, s_b1, z, nz, at_z)

    mine = core * nx + x
    done = piece_of(fin_a.at[mine], y)
    done[...] = sum_shared(copies_a, z_a, nz)
    copies_a = share(done, s_a[4], ny, at_y)
    x_b[x] = sum_dealt(m1_b[y], copies_b, r2_b)
    copies_b = share(x_b.at[x], s_b[2], nx, at_x)
    x_d[x] = sum_dealt(m1_d[z], copies_d, r2_d)
    copies_d = share(x_d.at[x], s_d[2], nx, at_x)
    b_y[y_hi] = sum_dealt(b_s[z], copies_bias, b_r1)
    copies_bias = share(b_y.at[y_hi], s_b2, ny_hi, at_yhi)

    for copy in copies_a:
        copy.wait()
    copies_a = share(fin_a.at[mine], s_a[5], nx, at_x)
    passed_a = [push(fin_a.at[mine], fin_a.at[mine], s_a[6], 0, at_core())]
    z_b[z] = sum_shared(copies_b, x_b, nx)
    copies_b = share(z_b.at[z], s_b[3], nz, at_z)
    z_d[y] = sum_shared(copies_d, x_d, nx)
    copies_d = share(z_d.at[y], s_d[3], ny, at_y)
    b_fin[z] = sum_shared(copies_bias, b_y, ny_hi)
    copies_bias = share(b_fin.at[z], s_b3, nz, at_z)

    def pass_on(fin, copies, sem, me, count):
        passed = []
        for j, copy in enumerate(copies, 1):
            copy.wait()
            got = fin.at[core * count + lax.rem(me - j + count, count)]
            passed.append(push(got, got, sem, j, at_core()))
        return passed

    def finish(copies, sem, fin, me, slots, count, others, where):
        own = fin.at[core * count + me]
        own[...] = sum_shared(copies, slots, others)
        passed = [push(own, own, sem[5], 0, at_core())]
        return share(own, sem[4], count, where), passed

    copies_b, passed_b = finish(copies_b, s_b, fin_b, y, z_b, ny, nz, at_y)
    copies_d, passed_d = finish(copies_d, s_d, fin_d, z, z_d, nz, ny, at_z)
    passed_a += pass_on(fin_a, copies_a, s_a[6], x, nx)

    stores = []

    def store(*which):
        for i in which:
            copy = pltpu.make_async_copy(ready[i], outs[i], out_sem.at[i])
            copy.start()
            stores.append(copy)

    def arrive(which, copies, out):
        for copy in copies:
            copy.wait()
        for half in range(2):
            for part in range(2):
                i = (1 - half) * 2 + 1 - part
                for row in range(3):
                    out[half * 3 + row, :, pl.ds(part * HALF, HALF)] = ex_r[
                        which, i, pl.ds(row * 2, 2), :
                    ].astype(BF16)

    arrive(0, exit_block, o_block)
    arrive(1, exit_token, o_token)

    store(0, 1)
    for copy in copies_bias:
        copy.wait()
    flat = b_fin[...].reshape(256, 128).astype(F32)
    for h in range(HEADS):
        o_bias[h, :, 0, 0:128] = flat[h * 24 : h * 24 + 23]
        o_bias[h, :, 0, 128:144] = flat[144:167, h * 16 : h * 16 + 16]
    store(5)
    passed_b += pass_on(fin_b, copies_b, s_b[5], y, ny)
    passed_d += pass_on(fin_d, copies_d, s_d[5], z, nz)

    scale = float(cells) ** (-0.5)

    def take(start, rows):
        parts = [
            fins[group][piece, pl.ds(row, count), :]
            for _, group, piece, row, count in flat_pieces(per, start, rows)
        ]
        whole = parts[0] if len(parts) == 1 else jnp.concatenate(parts, axis=0)
        return whole.astype(F32) * scale

    for copy in passed_a:
        copy.wait()
    for i in range(6):
        o_up[:, pl.ds(i * 128, 128)] = take(i * 192, 192)
    store(7)
    for copy in passed_b:
        copy.wait()
    for i in range(6):
        o_down[:, pl.ds(i * 128, 128)] = take(1152 + i * 192, 192)
    store(8)
    for copy in passed_d:
        copy.wait()
    for i in range(4):
        o_qkv[:, pl.ds(i * 128, 128)] = take(2304 + i * 192, 192)
    o_proj[:, 0:128] = take(3072, 192)
    rest = take(3264, 192)
    o_qkv[:, 512:576] = rest[:, :64]
    o_proj[:, 128:192] = rest[:, 64:]
    rest = take(3456, 16)
    o_n1[:, 0:128] = rest[0:1, :]
    o_n1[:, 128:192] = rest[1:2, :64]
    o_n2[:, 0:128] = rest[2:3, :]
    o_n2[:, 128:192] = rest[3:4, :64]
    store(2, 3, 4, 6)
    for copy in stores:
        copy.wait()


def piece_rows(geo):
    nlat, nlon, ny_lo, nx, nz, ny_hi = geo
    return ROWS[0] // (2 * nx), ROWS[1] // (2 * ny_lo * ny_hi), ROWS[2] // (2 * nz)


def spread(*refs):
    inputs, outs, held = refs[:9], refs[9:18], refs[18:27]
    sem_in, sem_out = refs[27:]
    order = (7, 8, 3, 5, 4, 0, 1, 2, 6)
    loads = [pltpu.make_async_copy(inputs[i], held[i], sem_in.at[i]) for i in range(9)]
    stores = [pltpu.make_async_copy(held[i], outs[i], sem_out.at[i]) for i in range(9)]
    for i in order:
        loads[i].start()
    for i in order:
        loads[i].wait()
        stores[i].start()
    for i in order:
        stores[i].wait()


def on_device(geo, tokens, labels, gain1, wqkv, wproj, table, gain2, wup, wdown, cotangent):
    nlat, nlon, ny_lo, nx, nz, ny_hi = geo
    ny = ny_lo * ny_hi
    pa, pb, pd = piece_rows(geo)
    rb = 256 // nz
    vmem = pltpu.VMEM
    args = (
        tokens.transpose(1, 0, 2), labels.transpose(1, 0, 2), gain1.reshape(1, C), wqkv, wproj,
        table.transpose(1, 2, 0, 3), gain2.reshape(1, C), wup, wdown.T, cotangent.transpose(1, 0, 2),
    )
    shape = jax.ShapeDtypeStruct
    shapes = (
        shape((6, 2, 12 * C), BF16),
        shape((6, 2, 12 * C), BF16),
        shape((1, C), F32),
        shape((C, 3 * C), F32),
        shape((C, C), F32),
        shape((HEADS, 23, 1, 144), F32),
        shape((1, C), F32),
        shape((C, FFN), F32),
        shape((C, FFN), F32),
    )
    scratch = [vmem(arg.shape, arg.dtype) for arg in args + shapes]
    scratch += [
        vmem((4, 16, HALF), F32),
        vmem((3, 16, HALF), BF16),
        vmem((3, 16, HALF), BF16),
        vmem((192, C), F32),
        vmem((192, C), F32),
        vmem((16, 128), F32),
        vmem((368, 192), F32),
        vmem((HEADS, 192, 192), F32),
        vmem((HEADS, 192, 192), F32),
        vmem((2, 4, 8, HALF), F32),
        vmem((2, 4, 8, HALF), F32),
        vmem((192, C), F32),
        vmem((16, 128), F32),
        vmem((HEADS, 192, 192), BF16),
        vmem((368, 192), BF16),
        vmem((HEADS, 24, 144), F32),
        vmem((256, 128), F32),
        vmem((nz, rb, 128), BF16),
        vmem((nz - 1, rb, 128), BF16),
        vmem((ny_hi, rb, 128), BF16),
        vmem((nz, rb, 128), BF16),
        vmem((2 * nx, pa, 128), BF16),
        vmem((nx, pa, 128), BF16),
        vmem((nx, pa, 128), BF16),
        vmem((nx - 1, pa, 128), BF16),
        vmem((pa, 128), BF16),
        vmem((ny - 1, pa // ny, 128), BF16),
        vmem((nz, pa // ny, 128), BF16),
        vmem((2 * nx, pa, 128), BF16),
    ]
    for first, piece, last in ((ny, pb, nz), (nz, pd, ny)):
        scratch += [
            vmem((2 * first, piece, 128), BF16),
            vmem((first, piece, 128), BF16),
            vmem((first, piece, 128), BF16),
            vmem((first - 1, piece, 128), BF16),
            vmem((nx, piece, 128), BF16),
            vmem((last, piece, 128), BF16),
            vmem((2 * first, piece, 128), BF16),
        ]
    scratch += [
        pltpu.SemaphoreType.DMA((10,)),
        pltpu.SemaphoreType.DMA((9,)),
    ]
    counts = [3, 3, 3, nz - 1, ny_hi - 1, nz - 1]
    counts += [1, nx - 1, ny - 1, nz - 1, ny - 1, nx - 1, nx]
    counts += [1, ny - 1, nx - 1, nz - 1, ny - 1, ny]
    counts += [1, nz - 1, nx - 1, ny - 1, nz - 1, nz]
    for count in counts:
        scratch += [pltpu.SemaphoreType.DMA((count,)), pltpu.SemaphoreType.DMA((count,))]
    anywhere = pl.BlockSpec(memory_space=pl.ANY)
    out = pl.pallas_call(
        functools.partial(kernel, geo),
        out_shape=shapes,
        in_specs=[anywhere] * 10,
        out_specs=(anywhere,) * 9,
        scratch_shapes=scratch,
        compiler_params=pltpu.CompilerParams(
            collective_id=0, has_side_effects=True, vmem_limit_bytes=63 * 1024 * 1024
        ),
    )(*args)
    out = pl.pallas_call(
        spread,
        out_shape=shapes,
        in_specs=[anywhere] * 9,
        out_specs=(anywhere,) * 9,
        scratch_shapes=[vmem(each.shape, each.dtype) for each in shapes]
        + [pltpu.SemaphoreType.DMA((9,)), pltpu.SemaphoreType.DMA((9,))],
        compiler_params=pltpu.CompilerParams(vmem_limit_bytes=63 * 1024 * 1024),
    )(*out)
    block, token, norm1, qkv, proj, bias, norm2, up, down = out
    return (
        block.transpose(1, 0, 2), token.transpose(1, 0, 2), norm1.reshape(C), qkv, proj,
        bias.transpose(2, 0, 1, 3), norm2.reshape(C), up, down.T,
    )


def geometry(mesh):
    nlat, nlon = mesh.shape["lat"], mesh.shape["lon"]
    ny_hi = 4 if nlon == 32 else 2
    nx = min(4, nlat // 2)
    return nlat, nlon, nlat // 2 // nx, nx, nlon // ny_hi, ny_hi


def solution(mesh):
    cells, band = P(None, "lat", "lon"), P("lat", None, None, None)
    return jax.shard_map(
        functools.partial(on_device, geometry(mesh)),
        mesh=mesh,
        in_specs=(cells, cells, P(), P(), P(), band, P(), P(), P(), cells),
        out_specs=(cells, cells, P(), P(), P(), band, P(), P(), P()),
        check_vma=False,
    )
```

```python
import functools

import jax
import jax.numpy as jnp
from jax import lax
from jax.experimental import pallas as pl
from jax.experimental.pallas import tpu as pltpu
from jax.sharding import PartitionSpec as P

MESH = pl.DeviceIdType.MESH
F32, BF16 = jnp.float32, jnp.bfloat16
C, HEADS, FFN = 192, 6, 768
HALF = 6 * C
EPS = 1e-05
COEFF = 0.044715
ROOT = 0.7978845608028654
MASKED = -1e30
SCALE = 32.0**-0.5
ROWS = (1024, 768, 768, 512, 512)
AT_UP, AT_DOWN, AT_PROJ, AT_QKV, AT_REST, AT_NORMS = 0, 1152, 2304, 2560, 3328, 3520
HOLD = 640


def nn(a, b):
    return jnp.dot(a, b, preferred_element_type=F32)


def nt(a, b):
    return lax.dot_general(a, b, (((1,), (1,)), ((), ())), preferred_element_type=F32)


def tn(a, b):
    return lax.dot_general(a, b, (((0,), (0,)), ((), ())), preferred_element_type=F32)


def mean(x):
    return jnp.sum(x, axis=-1, keepdims=True) * (1.0 / C)


def norm(x, gain):
    center = x - mean(x)
    inv = lax.rsqrt(mean(center * center) + EPS)
    xhat = center * inv
    return (xhat * gain).astype(BF16), xhat, inv


def norm_back(grad, xhat, inv, gain):
    g = grad * gain
    grad_in = inv * (g - mean(g) - xhat * mean(g * xhat))
    return grad_in, jnp.sum(grad * xhat, axis=0, keepdims=True)


def iota(shape, dim):
    return lax.broadcasted_iota(jnp.int32, shape, dim)


def cell_row(rho):
    half, r = rho >> 3, rho & 7
    return (r & 1) * 6 + half * 3 + (r >> 1), r < 6


def flat_pieces(sizes, start, rows):
    at = start
    while at < start + rows:
        group, base = 0, 0
        while at >= base + ROWS[group]:
            base += ROWS[group]
            group += 1
        per = sizes[group]
        inside = at - base
        take = min(per - inside % per, start + rows - at)
        yield at - start, group, inside // per, inside % per, take
        at += take


def kernel(
    geo, *refs,
):
    inputs, outs, held, ready, refs = refs[:10], refs[10:19], refs[19:29], refs[29:38], refs[38:]
    tok, lab, g1, wqkv, wproj, btab, g2, wup, wdown, cot = held
    o_block, o_token, o_n1, o_qkv, o_proj, o_bias, o_n2, o_up, o_down = ready
    (
        stage, ent_s, ent_r, xs, gs, labs, ytab, bias, probs, ex_s, ex_r, rows_st,
        nst, zfold, ffold, fsum, bst, b_s, b_r1, b_y, b_fin,
        buf_a, c_a, m1_a, r2_a, m2_a, r3_a, z_a, fin_a, *flat_refs,
    ) = refs[:57]
    in_sem, out_sem, *sems = refs[57:]
    loads = {}
    for i in (0, 9, 1, 5, 2, 3, 4, 6, 7, 8):
        loads[i] = pltpu.make_async_copy(inputs[i], held[i], in_sem.at[i])
        loads[i].start()
    nlat, nlon, ny_lo, nx, nz, ny_hi = geo
    ny = ny_lo * ny_hi
    per = piece_rows(geo)
    flat_refs = [flat_refs[7 * i : 7 * i + 7] for i in range(4)]
    bufs = (buf_a, *(each[0] for each in flat_refs))
    fins = (fin_a, *(each[6] for each in flat_refs))
    cells = 144 * nlat * nlon
    s_ent, s_ent2, s_exb, s_ext, s_b1, s_b2, s_b3, *s_groups = [
        (sems[2 * i], sems[2 * i + 1]) for i in range(len(sems) // 2)
    ]
    s_a = s_groups[:7]

    lat, lon = lax.axis_index("lat"), lax.axis_index("lon")
    core = lax.rem(lat, 2)
    x = lax.rem(lat // 2, nx)
    y_lo = lat // (2 * nx)
    z = lon // ny_hi
    y_hi = lax.rem(lon, ny_hi)
    y = y_hi * ny_lo + y_lo

    def at_core():
        return (lat + 1 - 2 * core, lon)

    def at_x(k):
        return ((y_lo * nx + lax.rem(x + k, nx)) * 2 + core, lon)

    def at_y(k):
        other = lax.rem(y + k, ny)
        return ((lax.rem(other, ny_lo) * nx + x) * 2 + core, z * ny_hi + other // ny_lo)

    def at_yhi(k):
        return (lat, z * ny_hi + lax.rem(y_hi + k, ny_hi))

    def at_z(k):
        return (lat, lax.rem(z + k, nz) * ny_hi + y_hi)

    def near(da, db):
        return (lax.rem(lat + da + nlat, nlat), lax.rem(lon + db + nlon, nlon))

    def push(src, dst, sem, i, dev):
        copy = pltpu.make_async_remote_copy(
            src_ref=src, dst_ref=dst, send_sem=sem[0].at[i], recv_sem=sem[1].at[i],
            device_id=dev, device_id_type=MESH,
        )
        copy.start()
        return copy

    barrier = pltpu.get_barrier_semaphore()
    partners = [at_core()]
    partners += [at_x(k) for k in range(1, nx)]
    partners += [at_y(k) for k in range(1, ny)]
    partners += [at_z(k) for k in range(1, nz)]
    partners += [near(-1, 0), near(0, -1), near(-1, -1), near(1, 0), near(0, 1), near(1, 1)]
    for dev in partners:
        pl.semaphore_signal(barrier, inc=1, device_id=dev, device_id_type=MESH)

    loads[0].wait()

    stage[...] = jnp.zeros_like(stage)

    def quarters(kind, ref):
        for half in range(2):
            for part in range(2):
                for row in range(3):
                    for side in range(2):
                        stage[kind, half * 2 + part, pl.ds(side * 8 + row * 2, 2), 0:576] = ref[
                            half * 3 + row, :, pl.ds(part * HALF + side * 576, 576)
                        ].astype(F32)
        for i in range(3):
            ent_s[kind, i] = stage[kind, i].astype(BF16)

    quarters(0, tok)
    pl.semaphore_wait(barrier, len(partners))
    places = ((0, 0), (0, 1), (1, 0))

    def enter(kind, sem):
        return [
            push(ent_s.at[kind, i], ent_r.at[kind, i], sem, i, near(half - 1, part - 1))
            for i, (half, part) in enumerate(places)
        ]

    entry = enter(0, s_ent)
    loads[9].wait()
    quarters(1, cot)
    entry2 = enter(1, s_ent2)

    loads[1].wait()
    loads[5].wait()

    labs[...] = jnp.full_like(labs, -1.0)
    for half in range(2):
        for row in range(3):
            labs[pl.ds(half * 8 + row * 2, 2), pl.ds(0, 12)] = lab[half * 3 + row].astype(F32)
    lab16 = labs[...].astype(BF16)
    pick = (11 - (iota((192, 128), 0) >> 4) == iota((192, 128), 1)).astype(F32).astype(BF16)
    lane_all = nt(lab16, pick)
    lane_lab = jnp.sum(
        jnp.where(iota((16, 192), 0) == (iota((16, 192), 1) & 15), lane_all, 0.0),
        axis=0, keepdims=True,
    )
    row_all = nt(pick, lab16)
    row_lab = jnp.sum(
        jnp.where(iota((192, 16), 1) == (iota((192, 16), 0) & 15), row_all, 0.0),
        axis=1, keepdims=True,
    )
    same = row_lab == lane_lab

    place, real = cell_row(iota((16, 144), 0))
    spot = iota((16, 144), 1)
    spot_row = (spot * 171) >> 11
    m1 = jnp.where((spot_row == place) & real, 1.0, 0.0)
    place_j, real_j = cell_row(iota((144, 192), 1) & 15)
    spot_j = iota((144, 192), 0)
    spot_col = spot_j - ((spot_j * 171) >> 11) * 12
    m2 = jnp.where((spot_col == place_j) & real_j, 1.0, 0.0).astype(BF16)
    group = iota((192, 192), 1) >> 4

    def build(h, carry):
        left = btab[h]
        full = jnp.zeros((368, 192), F32)
        for _ in range(3):
            piece = left.astype(BF16).astype(F32)
            left = left - piece
            wide = (piece * m1[None]).reshape(368, 144)
            full = full + nn(wide.astype(BF16), m2)
        ytab[...] = full
        out = ytab[pl.ds(176, 192), :]
        for bj in range(1, 12):
            out = jnp.where(group == bj, ytab[pl.ds((11 - bj) * 16, 192), :], out)
        bias[h] = jnp.where(same, out, MASKED)
        return carry

    lax.fori_loop(0, HEADS, build, 0)
    for i in (2, 4):
        bufs[i][...] = jnp.zeros_like(bufs[i])
    nst[...] = jnp.zeros_like(nst)
    bst[...] = jnp.zeros_like(bst)

    def lay(out, quarter, half, part):
        for c in range(6):
            row = (11 - part * 6 - c) * 16 + half * 8
            side, column = c // 3, c % 3
            out[pl.ds(row, 8), :] = quarter[side * 8 : side * 8 + 8, column * C : (column + 1) * C]

    def land(kind, out, copies):
        lay(out, stage[kind, 3], 0, 0)
        for i, (half, part) in enumerate(places):
            copies[i].wait()
            lay(out, ent_r[kind, i].astype(F32), 1 - half, 1 - part)

    for i in (2, 3, 4, 6, 7, 8):
        loads[i].wait()
    land(0, xs, entry)

    gain1, gain2 = g1[...], g2[...]
    tokens = xs[...]
    n1, xhat1, inv1 = norm(tokens, gain1)
    packed = nn(n1, wqkv[...]).astype(BF16)
    q, k, v = packed[:, :C], packed[:, C : 2 * C], packed[:, 2 * C :]
    head_of = iota((1, C), 1) >> 5
    masks = [(head_of == h).astype(F32).astype(BF16) for h in range(HEADS)]
    mixed = jnp.zeros((192, C), F32)
    for h in range(HEADS):
        s = nt(q * masks[h], k) * SCALE + bias[h]
        e = jnp.exp(s - jnp.max(s, axis=-1, keepdims=True))
        p = e * (1.0 / jnp.sum(e, axis=-1, keepdims=True))
        probs[h] = p
        mixed = mixed + nn(p.astype(BF16), v * masks[h])
    mixed = mixed.astype(BF16)
    branch = nn(mixed, wproj[...]).astype(BF16)
    residual = tokens + branch.astype(F32)
    n2, xhat2, inv2 = norm(residual, gain2)
    pre = nn(n2, wup[...])
    square = pre * pre
    tanh = jnp.tanh(ROOT * (pre + COEFF * pre * square))
    hidden = (0.5 * pre * (1.0 + tanh)).astype(BF16)
    slope = 0.5 * (1.0 + tanh) + 0.5 * pre * (1.0 - tanh * tanh) * ROOT * (
        1.0 + 3.0 * COEFF * square
    )
    block = residual + nt(hidden, wdown[...])

    def leave(which, value, sem):
        rows_st[...] = value
        copies = []
        for half in range(2):
            for part in range(2):
                i = half * 2 + part
                out = ex_r.at[which, 0] if i == 0 else ex_s.at[which, i]
                for c in range(6):
                    row = (11 - part * 6 - c) * 16 + half * 8
                    out[:, pl.ds(c * C, C)] = rows_st[pl.ds(row, 8), :]
                if i:
                    copies.append(
                        push(ex_s.at[which, i], ex_r.at[which, i], sem, i - 1, near(half, part))
                    )
        return copies

    exit_block = leave(0, block, s_exb)

    land(1, gs, entry2)
    grads = gs[...]
    grads16 = grads.astype(BF16)
    grad_pre = (nn(grads16, wdown[...]) * slope).astype(BF16)
    down = tn(grads16, hidden)
    up = tn(n2, grad_pre)

    def put(start, value, lanes=(0, 128)):
        value = value.astype(BF16)
        for src, group, piece, row, take in flat_pieces(per, start, value.shape[0]):
            bufs[group][piece, pl.ds(row, take), pl.ds(lanes[0], lanes[1] - lanes[0])] = value[
                src : src + take
            ]

    def half_to_core(buf, dst, sem, count):
        return push(buf.at[pl.ds((1 - core) * count, count)], dst, sem, 0, at_core())

    def own_half(buf, other, out, count, copy):
        copy.wait()
        for i in range(count):
            out[i] = (buf[core * count + i].astype(F32) + other[i].astype(F32)).astype(BF16)

    def deal(pieces, slots, sem, me, count, where):
        return [
            push(pieces(lax.rem(me + j, count)), slots.at[j - 1], sem, j - 1, where(j))
            for j in range(1, count)
        ]

    def share(ref, sem, count, where):
        return [push(ref, ref, sem, j - 1, where(j)) for j in range(1, count)]

    def sum_dealt(own, copies, slots):
        total = own.astype(F32)
        for i, copy in enumerate(copies):
            copy.wait()
            total = total + slots[i].astype(F32)
        return total.astype(BF16)

    def sum_shared(copies, slots, count):
        for copy in copies:
            copy.wait()
        total = slots[0].astype(F32)
        for i in range(1, count):
            total = total + slots[i].astype(F32)
        return total.astype(BF16)

    def pass_on(fin, copies, sem, me, count):
        passed = []
        for j, copy in enumerate(copies, 1):
            copy.wait()
            got = fin.at[core * count + lax.rem(me - j + count, count)]
            passed.append(push(got, got, sem, j, at_core()))
        return passed

    class Flat:
        def __init__(self, refs, sem, me, count, where, last, last_count, last_where):
            self.buf, self.c, self.m1, self.r2, self.x, self.z, self.fin = refs
            self.sem, self.me, self.count, self.where = sem, me, count, where
            self.last, self.last_count, self.last_where = last, last_count, last_where

        def start(self):
            self.copies = half_to_core(self.buf, self.c, self.sem[0], self.count)

        def deal(self):
            own_half(self.buf, self.c, self.m1, self.count, self.copies)
            self.copies = deal(
                lambda i: self.m1.at[i], self.r2, self.sem[1], self.me, self.count, self.where
            )

        def cross(self):
            self.x[x] = sum_dealt(self.m1[self.me], self.copies, self.r2)
            self.copies = share(self.x.at[x], self.sem[2], nx, at_x)

        def far(self):
            self.z[self.last] = sum_shared(self.copies, self.x, nx)
            self.copies = share(
                self.z.at[self.last], self.sem[3], self.last_count, self.last_where
            )

        def gather(self):
            own = self.fin.at[core * self.count + self.me]
            own[...] = sum_shared(self.copies, self.z, self.last_count)
            self.copies = share(own, self.sem[4], self.count, self.where)
            self.passed = [push(own, own, self.sem[5], 0, at_core())]

        def pass_on(self):
            self.passed += pass_on(self.fin, self.copies, self.sem[5], self.me, self.count)

        def wait(self):
            for copy in self.passed:
                copy.wait()

    ways = ((y, ny, at_y, z, nz, at_z), (z, nz, at_z, y, ny, at_y))
    early_y, early_z, late_y, late_z = [
        Flat(flat_refs[i], s_groups[7 + 6 * i : 13 + 6 * i], *ways[i % 2]) for i in range(4)
    ]

    for i in range(6):
        put(AT_UP + i * 192, up[:, i * 128 : (i + 1) * 128])
        put(AT_DOWN + i * 192, down[:, i * 128 : (i + 1) * 128])
    copies_a = half_to_core(buf_a, c_a, s_a[0], nx)
    early_y.start()

    grad_n2 = nt(grad_pre, wup[...])
    grad_in, norm2 = norm_back(grad_n2, xhat2, inv2, gain2)
    grad_res = grads + grad_in
    grad_branch = grad_res.astype(BF16)
    proj = tn(mixed, grad_branch)
    put(AT_PROJ, proj[:, :128])
    early_z.start()
    grad_mixed = nt(grad_branch, wproj[...]).astype(BF16)

    def piece_of(ref, index):
        size = per[0] // ny
        return ref.at[pl.ds(pl.multiple_of(index * size, 16), size)]

    dq = jnp.zeros((192, C), F32)
    dk = jnp.zeros((192, C), F32)
    dv = jnp.zeros((192, C), F32)
    for h in range(HEADS):
        gm = grad_mixed * masks[h]
        p = probs[h]
        dp = nt(gm, v)
        t = p * dp
        ds = ((t - p * jnp.sum(t, axis=-1, keepdims=True)) * SCALE).astype(BF16)
        zfold[h] = ds
        dv = dv + tn(p.astype(BF16), gm)
        dk = dk + tn(ds, q * masks[h])
        dq = dq + nn(ds, k * masks[h])
        if h == 0:
            own_half(buf_a, c_a, m1_a, nx, copies_a)
            copies_a = deal(lambda i: m1_a.at[i], r2_a, s_a[1], x, nx, at_x)
            early_y.deal()
        if h == 1:
            early_z.deal()
        if h == 5:
            m2_a[...] = sum_dealt(m1_a[x], copies_a, r2_a)
            copies_a = deal(lambda i: piece_of(m2_a, i), r3_a, s_a[2], y, ny, at_y)
    grad_packed = jnp.concatenate([dq, dk, dv], axis=1).astype(BF16)
    qkv = tn(n1, grad_packed)
    grad_n1 = nt(grad_packed, wqkv[...])
    grad_in1, norm1 = norm_back(grad_n1, xhat1, inv1, gain1)

    for i in range(4):
        put(AT_QKV + i * 192, qkv[:, i * 128 : (i + 1) * 128])
    put(AT_REST, qkv[:, 512:], (0, 64))
    put(AT_REST, proj[:, 128:], (64, 128))
    nst[0:1, :] = norm1[:, :128]
    nst[1:2, 0:64] = norm1[:, 128:]
    nst[2:3, :] = norm2[:, :128]
    nst[3:4, 0:64] = norm2[:, 128:]
    put(AT_NORMS, nst[...])
    late_y.start()
    late_z.start()

    token_grad = grad_res + grad_in1.astype(BF16).astype(F32)
    exit_token = leave(1, token_grad, s_ext)

    early_y.cross()
    early_z.cross()
    late_y.deal()
    late_z.deal()

    def fold(h, carry):
        ds = zfold[h]
        ffold[...] = jnp.zeros_like(ffold)
        for bj in range(12):
            one = (iota((1, 192), 1) >> 4 == bj).astype(F32).astype(BF16)
            ffold[pl.ds((11 - bj) * 16, 192), :] += ds * one
        wide = nt(ffold[...], m2).reshape(23, 16, 144) * m1[None]
        fsum[h, 0:23, :] = jnp.sum(wide, axis=1) * (1.0 / SCALE)
        return carry

    lax.fori_loop(0, HEADS, fold, 0)
    for h in range(HEADS):
        bst[pl.ds(h * 24, 23), :] = fsum[h, 0:23, 0:128]
        bst[pl.ds(144, 23), pl.ds(h * 16, 16)] = fsum[h, 0:23, 128:144]
    rb = 256 // nz
    b_s[...] = bst[...].astype(BF16).reshape(nz, rb, 128)
    copies_bias = deal(lambda i: b_s.at[i], b_r1, s_b1, z, nz, at_z)

    z_a[z] = sum_dealt(piece_of(m2_a, y)[...], copies_a, r3_a)
    copies_a = share(z_a.at[z], s_a[3], nz, at_z)
    early_y.far()
    early_z.far()
    late_y.cross()
    late_z.cross()
    b_y[y_hi] = sum_dealt(b_s[z], copies_bias, b_r1)
    copies_bias = share(b_y.at[y_hi], s_b2, ny_hi, at_yhi)
    mine = core * nx + x
    done = piece_of(fin_a.at[mine], y)
    done[...] = sum_shared(copies_a, z_a, nz)
    copies_a = share(done, s_a[4], ny, at_y)
    late_y.far()
    late_z.far()
    early_y.gather()
    early_z.gather()
    b_fin[z] = sum_shared(copies_bias, b_y, ny_hi)
    copies_bias = share(b_fin.at[z], s_b3, nz, at_z)
    for copy in copies_a:
        copy.wait()
    copies_a = share(fin_a.at[mine], s_a[5], nx, at_x)
    passed_a = [push(fin_a.at[mine], fin_a.at[mine], s_a[6], 0, at_core())]

    stores = []

    def store(*which):
        for i in which:
            copy = pltpu.make_async_copy(ready[i], outs[i], out_sem.at[i])
            copy.start()
            stores.append(copy)

    def arrive(which, copies, out):
        for copy in copies:
            copy.wait()
        for half in range(2):
            for part in range(2):
                i = (1 - half) * 2 + 1 - part
                for row in range(3):
                    out[half * 3 + row, :, pl.ds(part * HALF, HALF)] = ex_r[
                        which, i, pl.ds(row * 2, 2), :
                    ].astype(BF16)

    arrive(0, exit_block, o_block)
    arrive(1, exit_token, o_token)

    store(0, 1)
    late_y.gather()
    late_z.gather()
    for copy in copies_bias:
        copy.wait()
    flat = b_fin[...].reshape(256, 128).astype(F32)
    for h in range(HEADS):
        o_bias[h, :, 0, 0:128] = flat[h * 24 : h * 24 + 23]
        o_bias[h, :, 0, 128:144] = flat[144:167, h * 16 : h * 16 + 16]
    store(5)
    early_y.pass_on()
    early_z.pass_on()
    passed_a += pass_on(fin_a, copies_a, s_a[6], x, nx)

    scale = float(cells) ** (-0.5)

    def take(start, rows):
        parts = [
            fins[group][piece, pl.ds(row, count), :]
            for _, group, piece, row, count in flat_pieces(per, start, rows)
        ]
        whole = parts[0] if len(parts) == 1 else jnp.concatenate(parts, axis=0)
        return whole.astype(F32) * scale

    early_y.wait()
    early_z.wait()
    for copy in passed_a:
        copy.wait()
    for i in range(6):
        o_up[:, pl.ds(i * 128, 128)] = take(AT_UP + i * 192, 192)
    store(7)
    for i in range(6):
        o_down[:, pl.ds(i * 128, 128)] = take(AT_DOWN + i * 192, 192)
    store(8)
    o_proj[:, 0:128] = take(AT_PROJ, 192)
    late_y.pass_on()
    late_z.pass_on()
    late_y.wait()
    late_z.wait()
    for i in range(4):
        o_qkv[:, pl.ds(i * 128, 128)] = take(AT_QKV + i * 192, 192)
    rest = take(AT_REST, 192)
    o_qkv[:, 512:576] = rest[:, :64]
    o_proj[:, 128:192] = rest[:, 64:]
    rest = take(AT_NORMS, 16)
    o_n1[:, 0:128] = rest[0:1, :]
    o_n1[:, 128:192] = rest[1:2, :64]
    o_n2[:, 0:128] = rest[2:3, :]
    o_n2[:, 128:192] = rest[3:4, :64]
    store(2, 3, 4, 6)
    for copy in stores:
        copy.wait()


def piece_rows(geo):
    nlat, nlon, ny_lo, nx, nz, ny_hi = geo
    counts = (nx, ny_lo * ny_hi, nz, ny_lo * ny_hi, nz)
    return tuple(rows // (2 * count) for rows, count in zip(ROWS, counts))


def spread(*refs):
    inputs, outs, held = refs[:9], refs[9:18], refs[18:27]
    sem_in, sem_out = refs[27:]
    order = (7, 8, 3, 5, 4, 0, 1, 2, 6)
    loads = [pltpu.make_async_copy(inputs[i], held[i], sem_in.at[i]) for i in range(9)]
    stores = [pltpu.make_async_copy(held[i], outs[i], sem_out.at[i]) for i in range(9)]
    for i in order:
        loads[i].start()
    for i in order:
        loads[i].wait()
        stores[i].start()
    for i in order:
        stores[i].wait()


def on_device(geo, tokens, labels, gain1, wqkv, wproj, table, gain2, wup, wdown, cotangent):
    nlat, nlon, ny_lo, nx, nz, ny_hi = geo
    ny = ny_lo * ny_hi
    pa, *flat_rows = piece_rows(geo)
    rb = 256 // nz
    vmem = pltpu.VMEM
    args = (
        tokens.transpose(1, 0, 2), labels.transpose(1, 0, 2), gain1.reshape(1, C), wqkv, wproj,
        table.transpose(1, 2, 0, 3), gain2.reshape(1, C), wup, wdown.T, cotangent.transpose(1, 0, 2),
    )
    shape = jax.ShapeDtypeStruct
    shapes = (
        shape((6, 2, 12 * C), BF16),
        shape((6, 2, 12 * C), BF16),
        shape((1, C), F32),
        shape((C, 3 * C), F32),
        shape((C, C), F32),
        shape((HEADS, 23, 1, 144), F32),
        shape((1, C), F32),
        shape((C, FFN), F32),
        shape((C, FFN), F32),
    )
    scratch = [vmem(arg.shape, arg.dtype) for arg in args + shapes]
    scratch += [
        vmem((2, 4, 16, HOLD), F32),
        vmem((2, 3, 16, HOLD), BF16),
        vmem((2, 3, 16, HOLD), BF16),
        vmem((192, C), F32),
        vmem((192, C), F32),
        vmem((16, 128), F32),
        vmem((368, 192), F32),
        vmem((HEADS, 192, 192), F32),
        vmem((HEADS, 192, 192), F32),
        vmem((2, 4, 8, HALF), F32),
        vmem((2, 4, 8, HALF), F32),
        vmem((192, C), F32),
        vmem((16, 128), F32),
        vmem((HEADS, 192, 192), BF16),
        vmem((368, 192), BF16),
        vmem((HEADS, 24, 144), F32),
        vmem((256, 128), F32),
        vmem((nz, rb, 128), BF16),
        vmem((nz - 1, rb, 128), BF16),
        vmem((ny_hi, rb, 128), BF16),
        vmem((nz, rb, 128), BF16),
        vmem((2 * nx, pa, 128), BF16),
        vmem((nx, pa, 128), BF16),
        vmem((nx, pa, 128), BF16),
        vmem((nx - 1, pa, 128), BF16),
        vmem((pa, 128), BF16),
        vmem((ny - 1, pa // ny, 128), BF16),
        vmem((nz, pa // ny, 128), BF16),
        vmem((2 * nx, pa, 128), BF16),
    ]
    for piece, first, last in zip(flat_rows, (ny, nz, ny, nz), (nz, ny, nz, ny)):
        scratch += [
            vmem((2 * first, piece, 128), BF16),
            vmem((first, piece, 128), BF16),
            vmem((first, piece, 128), BF16),
            vmem((first - 1, piece, 128), BF16),
            vmem((nx, piece, 128), BF16),
            vmem((last, piece, 128), BF16),
            vmem((2 * first, piece, 128), BF16),
        ]
    scratch += [
        pltpu.SemaphoreType.DMA((10,)),
        pltpu.SemaphoreType.DMA((9,)),
    ]
    counts = [3, 3, 3, 3, nz - 1, ny_hi - 1, nz - 1]
    counts += [1, nx - 1, ny - 1, nz - 1, ny - 1, nx - 1, nx]
    for first, last in ((ny, nz), (nz, ny)) * 2:
        counts += [1, first - 1, nx - 1, last - 1, first - 1, first]
    for count in counts:
        scratch += [pltpu.SemaphoreType.DMA((count,)), pltpu.SemaphoreType.DMA((count,))]
    anywhere = pl.BlockSpec(memory_space=pl.ANY)
    out = pl.pallas_call(
        functools.partial(kernel, geo),
        out_shape=shapes,
        in_specs=[anywhere] * 10,
        out_specs=(anywhere,) * 9,
        scratch_shapes=scratch,
        compiler_params=pltpu.CompilerParams(
            collective_id=0, has_side_effects=True, vmem_limit_bytes=63 * 1024 * 1024
        ),
    )(*args)
    out = pl.pallas_call(
        spread,
        out_shape=shapes,
        in_specs=[anywhere] * 9,
        out_specs=(anywhere,) * 9,
        scratch_shapes=[vmem(each.shape, each.dtype) for each in shapes]
        + [pltpu.SemaphoreType.DMA((9,)), pltpu.SemaphoreType.DMA((9,))],
        compiler_params=pltpu.CompilerParams(vmem_limit_bytes=63 * 1024 * 1024),
    )(*out)
    block, token, norm1, qkv, proj, bias, norm2, up, down = out
    return (
        block.transpose(1, 0, 2), token.transpose(1, 0, 2), norm1.reshape(C), qkv, proj,
        bias.transpose(2, 0, 1, 3), norm2.reshape(C), up, down.T,
    )


def geometry(mesh):
    nlat, nlon = mesh.shape["lat"], mesh.shape["lon"]
    ny_hi = 4 if nlon == 32 else 2
    nx = min(4, nlat // 2)
    return nlat, nlon, nlat // 2 // nx, nx, nlon // ny_hi, ny_hi


def solution(mesh):
    cells, band = P(None, "lat", "lon"), P("lat", None, None, None)
    return jax.shard_map(
        functools.partial(on_device, geometry(mesh)),
        mesh=mesh,
        in_specs=(cells, cells, P(), P(), P(), band, P(), P(), P(), cells),
        out_specs=(cells, cells, P(), P(), P(), band, P(), P(), P()),
        check_vma=False,
    )
```

```python
import functools

import jax
import jax.numpy as jnp
from jax import lax
from jax.experimental import pallas as pl
from jax.experimental.pallas import tpu as pltpu
from jax.sharding import PartitionSpec as P

MESH = pl.DeviceIdType.MESH
F32, BF16 = jnp.float32, jnp.bfloat16
C, HEADS, FFN = 192, 6, 768
HALF = 6 * C
EPS = 1e-05
COEFF = 0.044715
ROOT = 0.7978845608028654
MASKED = -1e30
SCALE = 32.0**-0.5
ROWS = (1024, 768, 768, 512, 512)
AT_UP, AT_DOWN, AT_PROJ, AT_QKV, AT_REST, AT_NORMS = 0, 1152, 2304, 2560, 3328, 3520
HOLD = 640


def nn(a, b):
    return jnp.dot(a, b, preferred_element_type=F32)


def nt(a, b):
    return lax.dot_general(a, b, (((1,), (1,)), ((), ())), preferred_element_type=F32)


def tn(a, b):
    return lax.dot_general(a, b, (((0,), (0,)), ((), ())), preferred_element_type=F32)


def mean(x):
    return jnp.sum(x, axis=-1, keepdims=True) * (1.0 / C)


def norm(x, gain):
    center = x - mean(x)
    inv = lax.rsqrt(mean(center * center) + EPS)
    xhat = center * inv
    return (xhat * gain).astype(BF16), xhat, inv


def norm_back(grad, xhat, inv, gain):
    g = grad * gain
    grad_in = inv * (g - mean(g) - xhat * mean(g * xhat))
    return grad_in, jnp.sum(grad * xhat, axis=0, keepdims=True)


def iota(shape, dim):
    return lax.broadcasted_iota(jnp.int32, shape, dim)


def cell_row(rho):
    half, r = rho >> 3, rho & 7
    return (r & 1) * 6 + half * 3 + (r >> 1), r < 6


def flat_pieces(sizes, start, rows):
    at = start
    while at < start + rows:
        group, base = 0, 0
        while at >= base + ROWS[group]:
            base += ROWS[group]
            group += 1
        per = sizes[group]
        inside = at - base
        take = min(per - inside % per, start + rows - at)
        yield at - start, group, inside // per, inside % per, take
        at += take


def kernel(
    geo, *refs,
):
    inputs, outs, held, ready, refs = refs[:10], refs[10:19], refs[19:29], refs[29:38], refs[38:]
    tok, lab, g1, wqkv, wproj, btab, g2, wup, wdown, cot = held
    o_block, o_token, o_n1, o_qkv, o_proj, o_bias, o_n2, o_up, o_down = ready
    (
        stage, ent_s, ent_r, xs, gs, labs, ytab, bias, probs, ex_s, ex_r, rows_st,
        nst, zfold, ffold, fsum, bst, b_s, b_r1, b_y, b_fin,
        buf_a, c_a, m1_a, r2_a, m2_a, r3_a, z_a, fin_a, *flat_refs,
    ) = refs[:57]
    in_sem, out_sem, *sems = refs[57:]
    loads = {}
    for i in (0, 9, 1, 5, 2, 3, 4, 6, 7, 8):
        loads[i] = pltpu.make_async_copy(inputs[i], held[i], in_sem.at[i])
        loads[i].start()
    nlat, nlon, ny_lo, nx, nz, ny_hi = geo
    ny = ny_lo * ny_hi
    per = piece_rows(geo)
    flat_refs = [flat_refs[7 * i : 7 * i + 7] for i in range(4)]
    bufs = (buf_a, *(each[0] for each in flat_refs))
    fins = (fin_a, *(each[6] for each in flat_refs))
    cells = 144 * nlat * nlon
    s_ent, s_ent2, s_exb, s_ext, s_b1, s_b2, s_b3, *s_groups = [
        (sems[2 * i], sems[2 * i + 1]) for i in range(len(sems) // 2)
    ]
    s_a = s_groups[:7]

    lat, lon = lax.axis_index("lat"), lax.axis_index("lon")
    core = lax.rem(lat, 2)
    x = lax.rem(lat // 2, nx)
    y_lo = lat // (2 * nx)
    z = lon // ny_hi
    y_hi = lax.rem(lon, ny_hi)
    y = y_hi * ny_lo + y_lo

    def at_core():
        return (lat + 1 - 2 * core, lon)

    def at_x(k):
        return ((y_lo * nx + lax.rem(x + k, nx)) * 2 + core, lon)

    def at_y(k):
        other = lax.rem(y + k, ny)
        return ((lax.rem(other, ny_lo) * nx + x) * 2 + core, z * ny_hi + other // ny_lo)

    def at_yhi(k):
        return (lat, z * ny_hi + lax.rem(y_hi + k, ny_hi))

    def at_z(k):
        return (lat, lax.rem(z + k, nz) * ny_hi + y_hi)

    def near(da, db):
        return (lax.rem(lat + da + nlat, nlat), lax.rem(lon + db + nlon, nlon))

    def push(src, dst, sem, i, dev):
        copy = pltpu.make_async_remote_copy(
            src_ref=src, dst_ref=dst, send_sem=sem[0].at[i], recv_sem=sem[1].at[i],
            device_id=dev, device_id_type=MESH,
        )
        copy.start()
        return copy

    barrier = pltpu.get_barrier_semaphore()
    partners = [at_core()]
    partners += [at_x(k) for k in range(1, nx)]
    partners += [at_y(k) for k in range(1, ny)]
    partners += [at_z(k) for k in range(1, nz)]
    partners += [near(-1, 0), near(0, -1), near(-1, -1), near(1, 0), near(0, 1), near(1, 1)]
    for dev in partners:
        pl.semaphore_signal(barrier, inc=1, device_id=dev, device_id_type=MESH)

    loads[0].wait()

    stage[...] = jnp.zeros_like(stage)

    def quarters(kind, ref):
        for half in range(2):
            for part in range(2):
                for row in range(3):
                    for side in range(2):
                        stage[kind, half * 2 + part, pl.ds(side * 8 + row * 2, 2), 0:576] = ref[
                            half * 3 + row, :, pl.ds(part * HALF + side * 576, 576)
                        ].astype(F32)
        for i in range(3):
            ent_s[kind, i] = stage[kind, i].astype(BF16)

    quarters(0, tok)
    pl.semaphore_wait(barrier, len(partners))
    places = ((0, 0), (0, 1), (1, 0))

    def enter(kind, sem):
        return [
            push(ent_s.at[kind, i], ent_r.at[kind, i], sem, i, near(half - 1, part - 1))
            for i, (half, part) in enumerate(places)
        ]

    entry = enter(0, s_ent)
    loads[1].wait()
    loads[5].wait()

    labs[...] = jnp.full_like(labs, -1.0)
    for half in range(2):
        for row in range(3):
            labs[pl.ds(half * 8 + row * 2, 2), pl.ds(0, 12)] = lab[half * 3 + row].astype(F32)
    lab16 = labs[...].astype(BF16)
    pick = (11 - (iota((192, 128), 0) >> 4) == iota((192, 128), 1)).astype(F32).astype(BF16)
    lane_all = nt(lab16, pick)
    lane_lab = jnp.sum(
        jnp.where(iota((16, 192), 0) == (iota((16, 192), 1) & 15), lane_all, 0.0),
        axis=0, keepdims=True,
    )
    row_all = nt(pick, lab16)
    row_lab = jnp.sum(
        jnp.where(iota((192, 16), 1) == (iota((192, 16), 0) & 15), row_all, 0.0),
        axis=1, keepdims=True,
    )
    same = row_lab == lane_lab

    place, real = cell_row(iota((16, 144), 0))
    spot = iota((16, 144), 1)
    spot_row = (spot * 171) >> 11
    m1 = jnp.where((spot_row == place) & real, 1.0, 0.0)
    place_j, real_j = cell_row(iota((144, 192), 1) & 15)
    spot_j = iota((144, 192), 0)
    spot_col = spot_j - ((spot_j * 171) >> 11) * 12
    m2 = jnp.where((spot_col == place_j) & real_j, 1.0, 0.0).astype(BF16)
    group = iota((192, 192), 1) >> 4

    def build(h, carry):
        left = btab[h]
        full = jnp.zeros((368, 192), F32)
        for _ in range(3):
            piece = left.astype(BF16).astype(F32)
            left = left - piece
            wide = (piece * m1[None]).reshape(368, 144)
            full = full + nn(wide.astype(BF16), m2)
        ytab[...] = full
        out = ytab[pl.ds(176, 192), :]
        for bj in range(1, 12):
            out = jnp.where(group == bj, ytab[pl.ds((11 - bj) * 16, 192), :], out)
        bias[h] = jnp.where(same, out, MASKED)
        return carry

    lax.fori_loop(0, HEADS // 2, build, 0)
    loads[9].wait()
    quarters(1, cot)
    entry2 = enter(1, s_ent2)
    lax.fori_loop(HEADS // 2, HEADS, build, 0)
    for i in (2, 4):
        bufs[i][...] = jnp.zeros_like(bufs[i])
    nst[...] = jnp.zeros_like(nst)
    bst[...] = jnp.zeros_like(bst)

    def lay(out, quarter, half, part):
        for c in range(6):
            row = (11 - part * 6 - c) * 16 + half * 8
            side, column = c // 3, c % 3
            out[pl.ds(row, 8), :] = quarter[side * 8 : side * 8 + 8, column * C : (column + 1) * C]

    def land(kind, out, copies):
        lay(out, stage[kind, 3], 0, 0)
        for i, (half, part) in enumerate(places):
            copies[i].wait()
            lay(out, ent_r[kind, i].astype(F32), 1 - half, 1 - part)

    for i in (2, 3, 4, 6, 7, 8):
        loads[i].wait()
    land(0, xs, entry)

    gain1, gain2 = g1[...], g2[...]
    tokens = xs[...]
    n1, xhat1, inv1 = norm(tokens, gain1)
    packed = nn(n1, wqkv[...]).astype(BF16)
    q, k, v = packed[:, :C], packed[:, C : 2 * C], packed[:, 2 * C :]
    head_of = iota((1, C), 1) >> 5
    masks = [(head_of == h).astype(F32).astype(BF16) for h in range(HEADS)]
    mixed = jnp.zeros((192, C), F32)
    for h in range(HEADS):
        s = nt(q * masks[h], k) * SCALE + bias[h]
        e = jnp.exp(s - jnp.max(s, axis=-1, keepdims=True))
        p = e * (1.0 / jnp.sum(e, axis=-1, keepdims=True))
        probs[h] = p
        mixed = mixed + nn(p.astype(BF16), v * masks[h])
    mixed = mixed.astype(BF16)
    branch = nn(mixed, wproj[...]).astype(BF16)
    residual = tokens + branch.astype(F32)
    n2, xhat2, inv2 = norm(residual, gain2)
    pre = nn(n2, wup[...])
    square = pre * pre
    tanh = jnp.tanh(ROOT * (pre + COEFF * pre * square))
    hidden = (0.5 * pre * (1.0 + tanh)).astype(BF16)
    slope = 0.5 * (1.0 + tanh) + 0.5 * pre * (1.0 - tanh * tanh) * ROOT * (
        1.0 + 3.0 * COEFF * square
    )
    block = residual + nt(hidden, wdown[...])

    def leave(which, value, sem):
        rows_st[...] = value
        copies = []
        for half in range(2):
            for part in range(2):
                i = half * 2 + part
                out = ex_r.at[which, 0] if i == 0 else ex_s.at[which, i]
                for c in range(6):
                    row = (11 - part * 6 - c) * 16 + half * 8
                    out[:, pl.ds(c * C, C)] = rows_st[pl.ds(row, 8), :]
                if i:
                    copies.append(
                        push(ex_s.at[which, i], ex_r.at[which, i], sem, i - 1, near(half, part))
                    )
        return copies

    exit_block = leave(0, block, s_exb)

    land(1, gs, entry2)
    grads = gs[...]
    grads16 = grads.astype(BF16)
    grad_pre = (nn(grads16, wdown[...]) * slope).astype(BF16)
    down = tn(grads16, hidden)
    up = tn(n2, grad_pre)

    def put(start, value, lanes=(0, 128)):
        value = value.astype(BF16)
        for src, group, piece, row, take in flat_pieces(per, start, value.shape[0]):
            bufs[group][piece, pl.ds(row, take), pl.ds(lanes[0], lanes[1] - lanes[0])] = value[
                src : src + take
            ]

    def half_to_core(buf, dst, sem, count):
        return push(buf.at[pl.ds((1 - core) * count, count)], dst, sem, 0, at_core())

    def own_half(buf, other, out, count, copy):
        copy.wait()
        for i in range(count):
            out[i] = (buf[core * count + i].astype(F32) + other[i].astype(F32)).astype(BF16)

    def far_first(count):
        return sorted(range(1, count), key=lambda j: -min(j, count - j))

    def deal(pieces, slots, sem, me, count, where):
        return [
            push(pieces(lax.rem(me + j, count)), slots.at[j - 1], sem, j - 1, where(j))
            for j in far_first(count)
        ]

    def share(ref, sem, count, where):
        return [push(ref, ref, sem, j - 1, where(j)) for j in far_first(count)]

    def sum_dealt(own, copies, slots):
        total = own.astype(F32)
        for copy in copies:
            copy.wait()
        for i in range(len(copies)):
            total = total + slots[i].astype(F32)
        return total.astype(BF16)

    def sum_shared(copies, slots, count):
        for copy in copies:
            copy.wait()
        total = slots[0].astype(F32)
        for i in range(1, count):
            total = total + slots[i].astype(F32)
        return total.astype(BF16)

    def pass_on(fin, copies, sem, me, count):
        passed = []
        for j, copy in reversed(list(zip(far_first(count), copies))):
            copy.wait()
            got = fin.at[core * count + lax.rem(me - j + count, count)]
            passed.append(push(got, got, sem, j, at_core()))
        return passed

    class Flat:
        def __init__(self, refs, sem, me, count, where, last, last_count, last_where):
            self.buf, self.c, self.m1, self.r2, self.x, self.z, self.fin = refs
            self.sem, self.me, self.count, self.where = sem, me, count, where
            self.last, self.last_count, self.last_where = last, last_count, last_where

        def start(self):
            self.copies = half_to_core(self.buf, self.c, self.sem[0], self.count)

        def deal(self):
            own_half(self.buf, self.c, self.m1, self.count, self.copies)
            self.copies = deal(
                lambda i: self.m1.at[i], self.r2, self.sem[1], self.me, self.count, self.where
            )

        def cross(self):
            self.x[x] = sum_dealt(self.m1[self.me], self.copies, self.r2)
            self.copies = share(self.x.at[x], self.sem[2], nx, at_x)

        def far(self):
            self.z[self.last] = sum_shared(self.copies, self.x, nx)
            self.copies = share(
                self.z.at[self.last], self.sem[3], self.last_count, self.last_where
            )

        def gather(self):
            own = self.fin.at[core * self.count + self.me]
            own[...] = sum_shared(self.copies, self.z, self.last_count)
            self.copies = share(own, self.sem[4], self.count, self.where)
            self.passed = [push(own, own, self.sem[5], 0, at_core())]

        def pass_on(self):
            self.passed += pass_on(self.fin, self.copies, self.sem[5], self.me, self.count)

        def wait(self):
            for copy in self.passed:
                copy.wait()

    ways = ((y, ny, at_y, z, nz, at_z), (z, nz, at_z, y, ny, at_y))
    early_y, early_z, late_y, late_z = [
        Flat(flat_refs[i], s_groups[7 + 6 * i : 13 + 6 * i], *ways[i % 2]) for i in range(4)
    ]

    for i in range(6):
        put(AT_UP + i * 192, up[:, i * 128 : (i + 1) * 128])
        put(AT_DOWN + i * 192, down[:, i * 128 : (i + 1) * 128])
    copies_a = half_to_core(buf_a, c_a, s_a[0], nx)
    early_y.start()

    grad_n2 = nt(grad_pre, wup[...])
    grad_in, norm2 = norm_back(grad_n2, xhat2, inv2, gain2)
    grad_res = grads + grad_in
    grad_branch = grad_res.astype(BF16)
    proj = tn(mixed, grad_branch)
    put(AT_PROJ, proj[:, :128])
    early_z.start()
    grad_mixed = nt(grad_branch, wproj[...]).astype(BF16)

    def piece_of(ref, index):
        size = per[0] // ny
        return ref.at[pl.ds(pl.multiple_of(index * size, 16), size)]

    dq = jnp.zeros((192, C), F32)
    dk = jnp.zeros((192, C), F32)
    dv = jnp.zeros((192, C), F32)
    for h in range(HEADS):
        gm = grad_mixed * masks[h]
        p = probs[h]
        dp = nt(gm, v)
        t = p * dp
        ds = ((t - p * jnp.sum(t, axis=-1, keepdims=True)) * SCALE).astype(BF16)
        zfold[h] = ds
        dv = dv + tn(p.astype(BF16), gm)
        dk = dk + tn(ds, q * masks[h])
        dq = dq + nn(ds, k * masks[h])
        if h == 2:
            own_half(buf_a, c_a, m1_a, nx, copies_a)
            copies_a = deal(lambda i: m1_a.at[i], r2_a, s_a[1], x, nx, at_x)
            early_y.deal()
        if h == 5:
            early_z.deal()
    grad_packed = jnp.concatenate([dq, dk, dv], axis=1).astype(BF16)
    qkv = tn(n1, grad_packed)
    grad_n1 = nt(grad_packed, wqkv[...])
    grad_in1, norm1 = norm_back(grad_n1, xhat1, inv1, gain1)

    for i in range(4):
        put(AT_QKV + i * 192, qkv[:, i * 128 : (i + 1) * 128])
    put(AT_REST, qkv[:, 512:], (0, 64))
    put(AT_REST, proj[:, 128:], (64, 128))
    nst[0:1, :] = norm1[:, :128]
    nst[1:2, 0:64] = norm1[:, 128:]
    nst[2:3, :] = norm2[:, :128]
    nst[3:4, 0:64] = norm2[:, 128:]
    put(AT_NORMS, nst[...])
    late_y.start()
    late_z.start()

    token_grad = grad_res + grad_in1.astype(BF16).astype(F32)
    exit_token = leave(1, token_grad, s_ext)

    def fold(h, carry):
        ds = zfold[h]
        ffold[...] = jnp.zeros_like(ffold)
        for bj in range(12):
            one = (iota((1, 192), 1) >> 4 == bj).astype(F32).astype(BF16)
            ffold[pl.ds((11 - bj) * 16, 192), :] += ds * one
        wide = nt(ffold[...], m2).reshape(23, 16, 144) * m1[None]
        fsum[h, 0:23, :] = jnp.sum(wide, axis=1) * (1.0 / SCALE)
        return carry

    lax.fori_loop(0, HEADS // 2, fold, 0)
    late_y.deal()
    late_z.deal()
    m2_a[...] = sum_dealt(m1_a[x], copies_a, r2_a)
    copies_a = deal(lambda i: piece_of(m2_a, i), r3_a, s_a[2], y, ny, at_y)
    early_y.cross()
    early_z.cross()
    lax.fori_loop(HEADS // 2, HEADS, fold, 0)
    for h in range(HEADS):
        bst[pl.ds(h * 24, 23), :] = fsum[h, 0:23, 0:128]
        bst[pl.ds(144, 23), pl.ds(h * 16, 16)] = fsum[h, 0:23, 128:144]
    rb = 256 // nz
    b_s[...] = bst[...].astype(BF16).reshape(nz, rb, 128)
    copies_bias = deal(lambda i: b_s.at[i], b_r1, s_b1, z, nz, at_z)

    z_a[z] = sum_dealt(piece_of(m2_a, y)[...], copies_a, r3_a)
    copies_a = share(z_a.at[z], s_a[3], nz, at_z)
    late_y.cross()
    late_z.cross()
    early_y.far()
    early_z.far()
    b_y[y_hi] = sum_dealt(b_s[z], copies_bias, b_r1)
    copies_bias = share(b_y.at[y_hi], s_b2, ny_hi, at_yhi)
    mine = core * nx + x
    done = piece_of(fin_a.at[mine], y)
    done[...] = sum_shared(copies_a, z_a, nz)
    copies_a = share(done, s_a[4], ny, at_y)
    late_y.far()
    late_z.far()
    early_y.gather()
    early_z.gather()
    b_fin[z] = sum_shared(copies_bias, b_y, ny_hi)
    copies_bias = share(b_fin.at[z], s_b3, nz, at_z)
    stores = []

    def store(*which):
        for i in which:
            copy = pltpu.make_async_copy(ready[i], outs[i], out_sem.at[i])
            copy.start()
            stores.append(copy)

    def arrive(which, copies, out):
        for copy in copies:
            copy.wait()
        for half in range(2):
            for part in range(2):
                i = (1 - half) * 2 + 1 - part
                for row in range(3):
                    out[half * 3 + row, :, pl.ds(part * HALF, HALF)] = ex_r[
                        which, i, pl.ds(row * 2, 2), :
                    ].astype(BF16)

    arrive(0, exit_block, o_block)
    arrive(1, exit_token, o_token)

    store(0, 1)
    late_y.gather()
    late_z.gather()
    for copy in copies_a:
        copy.wait()
    copies_a = share(fin_a.at[mine], s_a[5], nx, at_x)
    passed_a = [push(fin_a.at[mine], fin_a.at[mine], s_a[6], 0, at_core())]
    for copy in copies_bias:
        copy.wait()
    flat = b_fin[...].reshape(256, 128).astype(F32)
    for h in range(HEADS):
        o_bias[h, :, 0, 0:128] = flat[h * 24 : h * 24 + 23]
        o_bias[h, :, 0, 128:144] = flat[144:167, h * 16 : h * 16 + 16]
    store(5)
    early_y.pass_on()
    early_z.pass_on()
    passed_a += pass_on(fin_a, copies_a, s_a[6], x, nx)
    late_y.pass_on()
    late_z.pass_on()

    scale = float(cells) ** (-0.5)

    def take(start, rows):
        parts = [
            fins[group][piece, pl.ds(row, count), :]
            for _, group, piece, row, count in flat_pieces(per, start, rows)
        ]
        whole = parts[0] if len(parts) == 1 else jnp.concatenate(parts, axis=0)
        return whole.astype(F32) * scale

    early_y.wait()
    early_z.wait()
    for copy in passed_a:
        copy.wait()
    for i in range(6):
        o_up[:, pl.ds(i * 128, 128)] = take(AT_UP + i * 192, 192)
    store(7)
    for i in range(6):
        o_down[:, pl.ds(i * 128, 128)] = take(AT_DOWN + i * 192, 192)
    store(8)
    o_proj[:, 0:128] = take(AT_PROJ, 192)
    late_y.wait()
    late_z.wait()
    for i in range(4):
        o_qkv[:, pl.ds(i * 128, 128)] = take(AT_QKV + i * 192, 192)
    rest = take(AT_REST, 192)
    o_qkv[:, 512:576] = rest[:, :64]
    o_proj[:, 128:192] = rest[:, 64:]
    rest = take(AT_NORMS, 16)
    o_n1[:, 0:128] = rest[0:1, :]
    o_n1[:, 128:192] = rest[1:2, :64]
    o_n2[:, 0:128] = rest[2:3, :]
    o_n2[:, 128:192] = rest[3:4, :64]
    store(2, 3, 4, 6)
    for copy in stores:
        copy.wait()


def piece_rows(geo):
    nlat, nlon, ny_lo, nx, nz, ny_hi = geo
    counts = (nx, ny_lo * ny_hi, nz, ny_lo * ny_hi, nz)
    return tuple(rows // (2 * count) for rows, count in zip(ROWS, counts))


def spread(*refs):
    inputs, outs, held = refs[:9], refs[9:18], refs[18:27]
    sem_in, sem_out = refs[27:]
    order = (7, 8, 3, 5, 4, 0, 1, 2, 6)
    loads = [pltpu.make_async_copy(inputs[i], held[i], sem_in.at[i]) for i in range(9)]
    stores = [pltpu.make_async_copy(held[i], outs[i], sem_out.at[i]) for i in range(9)]
    for i in order:
        loads[i].start()
    for i in order:
        loads[i].wait()
        stores[i].start()
    for i in order:
        stores[i].wait()


def on_device(geo, tokens, labels, gain1, wqkv, wproj, table, gain2, wup, wdown, cotangent):
    nlat, nlon, ny_lo, nx, nz, ny_hi = geo
    ny = ny_lo * ny_hi
    pa, *flat_rows = piece_rows(geo)
    rb = 256 // nz
    vmem = pltpu.VMEM
    args = (
        tokens.transpose(1, 0, 2), labels.transpose(1, 0, 2), gain1.reshape(1, C), wqkv, wproj,
        table.transpose(1, 2, 0, 3), gain2.reshape(1, C), wup, wdown.T, cotangent.transpose(1, 0, 2),
    )
    shape = jax.ShapeDtypeStruct
    shapes = (
        shape((6, 2, 12 * C), BF16),
        shape((6, 2, 12 * C), BF16),
        shape((1, C), F32),
        shape((C, 3 * C), F32),
        shape((C, C), F32),
        shape((HEADS, 23, 1, 144), F32),
        shape((1, C), F32),
        shape((C, FFN), F32),
        shape((C, FFN), F32),
    )
    scratch = [vmem(arg.shape, arg.dtype) for arg in args + shapes]
    scratch += [
        vmem((2, 4, 16, HOLD), F32),
        vmem((2, 3, 16, HOLD), BF16),
        vmem((2, 3, 16, HOLD), BF16),
        vmem((192, C), F32),
        vmem((192, C), F32),
        vmem((16, 128), F32),
        vmem((368, 192), F32),
        vmem((HEADS, 192, 192), F32),
        vmem((HEADS, 192, 192), F32),
        vmem((2, 4, 8, HALF), F32),
        vmem((2, 4, 8, HALF), F32),
        vmem((192, C), F32),
        vmem((16, 128), F32),
        vmem((HEADS, 192, 192), BF16),
        vmem((368, 192), BF16),
        vmem((HEADS, 24, 144), F32),
        vmem((256, 128), F32),
        vmem((nz, rb, 128), BF16),
        vmem((nz - 1, rb, 128), BF16),
        vmem((ny_hi, rb, 128), BF16),
        vmem((nz, rb, 128), BF16),
        vmem((2 * nx, pa, 128), BF16),
        vmem((nx, pa, 128), BF16),
        vmem((nx, pa, 128), BF16),
        vmem((nx - 1, pa, 128), BF16),
        vmem((pa, 128), BF16),
        vmem((ny - 1, pa // ny, 128), BF16),
        vmem((nz, pa // ny, 128), BF16),
        vmem((2 * nx, pa, 128), BF16),
    ]
    for piece, first, last in zip(flat_rows, (ny, nz, ny, nz), (nz, ny, nz, ny)):
        scratch += [
            vmem((2 * first, piece, 128), BF16),
            vmem((first, piece, 128), BF16),
            vmem((first, piece, 128), BF16),
            vmem((first - 1, piece, 128), BF16),
            vmem((nx, piece, 128), BF16),
            vmem((last, piece, 128), BF16),
            vmem((2 * first, piece, 128), BF16),
        ]
    scratch += [
        pltpu.SemaphoreType.DMA((10,)),
        pltpu.SemaphoreType.DMA((9,)),
    ]
    counts = [3, 3, 3, 3, nz - 1, ny_hi - 1, nz - 1]
    counts += [1, nx - 1, ny - 1, nz - 1, ny - 1, nx - 1, nx]
    for first, last in ((ny, nz), (nz, ny)) * 2:
        counts += [1, first - 1, nx - 1, last - 1, first - 1, first]
    for count in counts:
        scratch += [pltpu.SemaphoreType.DMA((count,)), pltpu.SemaphoreType.DMA((count,))]
    anywhere = pl.BlockSpec(memory_space=pl.ANY)
    out = pl.pallas_call(
        functools.partial(kernel, geo),
        out_shape=shapes,
        in_specs=[anywhere] * 10,
        out_specs=(anywhere,) * 9,
        scratch_shapes=scratch,
        compiler_params=pltpu.CompilerParams(
            collective_id=0, has_side_effects=True, vmem_limit_bytes=63 * 1024 * 1024
        ),
    )(*args)
    out = pl.pallas_call(
        spread,
        out_shape=shapes,
        in_specs=[anywhere] * 9,
        out_specs=(anywhere,) * 9,
        scratch_shapes=[vmem(each.shape, each.dtype) for each in shapes]
        + [pltpu.SemaphoreType.DMA((9,)), pltpu.SemaphoreType.DMA((9,))],
        compiler_params=pltpu.CompilerParams(vmem_limit_bytes=63 * 1024 * 1024),
    )(*out)
    block, token, norm1, qkv, proj, bias, norm2, up, down = out
    return (
        block.transpose(1, 0, 2), token.transpose(1, 0, 2), norm1.reshape(C), qkv, proj,
        bias.transpose(2, 0, 1, 3), norm2.reshape(C), up, down.T,
    )


def geometry(mesh):
    nlat, nlon = mesh.shape["lat"], mesh.shape["lon"]
    ny_hi = 4 if nlon == 32 else 2
    nx = min(4, nlat // 2)
    return nlat, nlon, nlat // 2 // nx, nx, nlon // ny_hi, ny_hi


def solution(mesh):
    cells, band = P(None, "lat", "lon"), P("lat", None, None, None)
    return jax.shard_map(
        functools.partial(on_device, geometry(mesh)),
        mesh=mesh,
        in_specs=(cells, cells, P(), P(), P(), band, P(), P(), P(), cells),
        out_specs=(cells, cells, P(), P(), P(), band, P(), P(), P()),
        check_vma=False,
    )
```

```python
import functools

import jax
import jax.numpy as jnp
from jax import lax
from jax.experimental import pallas as pl
from jax.experimental.pallas import tpu as pltpu
from jax.sharding import PartitionSpec as P

MESH = pl.DeviceIdType.MESH
F32, BF16 = jnp.float32, jnp.bfloat16
C, HEADS, FFN = 192, 6, 768
HALF = 6 * C
EPS = 1e-05
COEFF = 0.044715
ROOT = 0.7978845608028654
MASKED = -1e30
SCALE = 32.0**-0.5
ROWS = (1024, 768, 768, 512, 512)
AT_UP, AT_DOWN, AT_PROJ, AT_QKV, AT_REST, AT_NORMS = 0, 1152, 2304, 2560, 3328, 3520
HOLD = 640


def nn(a, b):
    return jnp.dot(a, b, preferred_element_type=F32)


def nt(a, b):
    return lax.dot_general(a, b, (((1,), (1,)), ((), ())), preferred_element_type=F32)


def tn(a, b):
    return lax.dot_general(a, b, (((0,), (0,)), ((), ())), preferred_element_type=F32)


def mean(x):
    return jnp.sum(x, axis=-1, keepdims=True) * (1.0 / C)


def norm(x, gain):
    center = x - mean(x)
    inv = lax.rsqrt(mean(center * center) + EPS)
    xhat = center * inv
    return (xhat * gain).astype(BF16), xhat, inv


def norm_back(grad, xhat, inv, gain):
    g = grad * gain
    grad_in = inv * (g - mean(g) - xhat * mean(g * xhat))
    return grad_in, jnp.sum(grad * xhat, axis=0, keepdims=True)


def iota(shape, dim):
    return lax.broadcasted_iota(jnp.int32, shape, dim)


def cell_row(rho):
    half, r = rho >> 3, rho & 7
    return (r & 1) * 6 + half * 3 + (r >> 1), r < 6


def flat_pieces(sizes, start, rows):
    at = start
    while at < start + rows:
        group, base = 0, 0
        while at >= base + ROWS[group]:
            base += ROWS[group]
            group += 1
        per = sizes[group]
        inside = at - base
        take = min(per - inside % per, start + rows - at)
        yield at - start, group, inside // per, inside % per, take
        at += take


def kernel(
    geo, *refs,
):
    inputs, outs, held, ready, refs = refs[:10], refs[10:19], refs[19:29], refs[29:38], refs[38:]
    tok, lab, g1, wqkv, wproj, btab, g2, wup, wdown, cot = held
    o_block, o_token, o_n1, o_qkv, o_proj, o_bias, o_n2, o_up, o_down = ready
    (
        stage, ent_s, ent_r, xs, gs, labs, ytab, bias, probs, ex_st, ex_s, ex_r, rows_st,
        nst, zfold, ffold, fsum, bst, b_s, b_r1, b_y, b_fin,
        buf_a, c_a, m1_a, r2_a, m2_a, r3_a, z_a, fin_a, *flat_refs,
    ) = refs[:58]
    in_sem, out_sem, *sems = refs[58:]
    nlat, nlon, ny_lo, nx, nz, ny_hi = geo
    ny = ny_lo * ny_hi
    per = piece_rows(geo)
    flat_refs = [flat_refs[7 * i : 7 * i + 7] for i in range(4)]
    bufs = (buf_a, *(each[0] for each in flat_refs))
    fins = (fin_a, *(each[6] for each in flat_refs))
    cells = 144 * nlat * nlon
    s_ent, s_ent2, s_exb, s_ext, s_b1, s_b2, s_b3, *s_groups = [
        (sems[2 * i], sems[2 * i + 1]) for i in range(len(sems) // 2)
    ]
    s_a = s_groups[:7]

    lat, lon = lax.axis_index("lat"), lax.axis_index("lon")
    core = lax.rem(lat, 2)
    x = lax.rem(lat // 2, nx)
    y_lo = lat // (2 * nx)
    z = lon // ny_hi
    y_hi = lax.rem(lon, ny_hi)
    y = y_hi * ny_lo + y_lo

    def at_core():
        return (lat + 1 - 2 * core, lon)

    def at_x(k):
        return ((y_lo * nx + lax.rem(x + k, nx)) * 2 + core, lon)

    def at_y(k):
        other = lax.rem(y + k, ny)
        return ((lax.rem(other, ny_lo) * nx + x) * 2 + core, z * ny_hi + other // ny_lo)

    def at_yhi(k):
        return (lat, z * ny_hi + lax.rem(y_hi + k, ny_hi))

    def at_z(k):
        return (lat, lax.rem(z + k, nz) * ny_hi + y_hi)

    def near(da, db):
        return (lax.rem(lat + da + nlat, nlat), lax.rem(lon + db + nlon, nlon))

    def push(src, dst, sem, i, dev):
        copy = pltpu.make_async_remote_copy(
            src_ref=src, dst_ref=dst, send_sem=sem[0].at[i], recv_sem=sem[1].at[i],
            device_id=dev, device_id_type=MESH,
        )
        copy.start()
        return copy

    barrier = pltpu.get_barrier_semaphore()
    partners = [near(-1, 0), near(0, -1), near(-1, -1), near(1, 0), near(0, 1), near(1, 1)]
    partners += [at_core()]
    partners += [at_x(k) for k in range(1, nx)]
    partners += [at_y(k) for k in range(1, ny)]
    partners += [at_z(k) for k in range(1, nz)]
    for dev in partners:
        pl.semaphore_signal(barrier, inc=1, device_id=dev, device_id_type=MESH)
    loads = {}
    for i in (0, 9, 1, 5, 2, 3, 4, 6, 7, 8):
        loads[i] = pltpu.make_async_copy(inputs[i], held[i], in_sem.at[i])
        loads[i].start()

    loads[0].wait()

    stage[...] = jnp.zeros_like(stage)
    ex_st[...] = jnp.zeros_like(ex_st)

    def quarters(kind, ref):
        for half in range(2):
            for part in range(2):
                for row in range(3):
                    for side in range(2):
                        stage[kind, half * 2 + part, pl.ds(side * 8 + row * 2, 2), 0:576] = ref[
                            half * 3 + row, :, pl.ds(part * HALF + side * 576, 576)
                        ].astype(F32)
        for i in range(3):
            ent_s[kind, i] = stage[kind, i].astype(BF16)

    quarters(0, tok)
    pl.semaphore_wait(barrier, len(partners))
    places = ((0, 0), (0, 1), (1, 0))

    def enter(kind, sem):
        return [
            push(ent_s.at[kind, i], ent_r.at[kind, i], sem, i, near(half - 1, part - 1))
            for i, (half, part) in enumerate(places)
        ]

    entry = enter(0, s_ent)
    loads[1].wait()
    loads[5].wait()

    labs[...] = jnp.full_like(labs, -1.0)
    for half in range(2):
        for row in range(3):
            labs[pl.ds(half * 8 + row * 2, 2), pl.ds(0, 12)] = lab[half * 3 + row].astype(F32)
    lab16 = labs[...].astype(BF16)
    pick = (11 - (iota((192, 128), 0) >> 4) == iota((192, 128), 1)).astype(F32).astype(BF16)
    lane_all = nt(lab16, pick)
    lane_lab = jnp.sum(
        jnp.where(iota((16, 192), 0) == (iota((16, 192), 1) & 15), lane_all, 0.0),
        axis=0, keepdims=True,
    )
    row_all = nt(pick, lab16)
    row_lab = jnp.sum(
        jnp.where(iota((192, 16), 1) == (iota((192, 16), 0) & 15), row_all, 0.0),
        axis=1, keepdims=True,
    )
    same = row_lab == lane_lab

    place, real = cell_row(iota((16, 144), 0))
    spot = iota((16, 144), 1)
    spot_row = (spot * 171) >> 11
    m1 = jnp.where((spot_row == place) & real, 1.0, 0.0)
    place_j, real_j = cell_row(iota((144, 192), 1) & 15)
    spot_j = iota((144, 192), 0)
    spot_col = spot_j - ((spot_j * 171) >> 11) * 12
    m2 = jnp.where((spot_col == place_j) & real_j, 1.0, 0.0).astype(BF16)
    group = iota((192, 192), 1) >> 4

    def build(h, carry):
        left = btab[h]
        full = jnp.zeros((368, 192), F32)
        for _ in range(3):
            piece = left.astype(BF16).astype(F32)
            left = left - piece
            wide = (piece * m1[None]).reshape(368, 144)
            full = full + nn(wide.astype(BF16), m2)
        ytab[...] = full
        out = ytab[pl.ds(176, 192), :]
        for bj in range(1, 12):
            out = jnp.where(group == bj, ytab[pl.ds((11 - bj) * 16, 192), :], out)
        bias[h] = jnp.where(same, out, MASKED)
        return carry

    lax.fori_loop(0, HEADS // 2, build, 0)
    loads[9].wait()
    quarters(1, cot)
    entry2 = enter(1, s_ent2)
    lax.fori_loop(HEADS // 2, HEADS, build, 0)
    for i in (2, 4):
        bufs[i][...] = jnp.zeros_like(bufs[i])
    nst[...] = jnp.zeros_like(nst)
    bst[...] = jnp.zeros_like(bst)

    def lay(out, quarter, half, part):
        for c in range(6):
            row = (11 - part * 6 - c) * 16 + half * 8
            side, column = c // 3, c % 3
            out[pl.ds(row, 8), :] = quarter[side * 8 : side * 8 + 8, column * C : (column + 1) * C]

    def land(kind, out, copies):
        lay(out, stage[kind, 3], 0, 0)
        for i, (half, part) in enumerate(places):
            copies[i].wait()
            lay(out, ent_r[kind, i].astype(F32), 1 - half, 1 - part)

    for i in (2, 3, 4, 6, 7, 8):
        loads[i].wait()
    land(0, xs, entry)

    gain1, gain2 = g1[...], g2[...]
    tokens = xs[...]
    n1, xhat1, inv1 = norm(tokens, gain1)
    packed = nn(n1, wqkv[...]).astype(BF16)
    q, k, v = packed[:, :C], packed[:, C : 2 * C], packed[:, 2 * C :]
    head_of = iota((1, C), 1) >> 5
    masks = [(head_of == h).astype(F32).astype(BF16) for h in range(HEADS)]
    mixed = jnp.zeros((192, C), F32)
    for h in range(HEADS):
        s = nt(q * masks[h], k) * SCALE + bias[h]
        e = jnp.exp(s - jnp.max(s, axis=-1, keepdims=True))
        p = e * (1.0 / jnp.sum(e, axis=-1, keepdims=True))
        probs[h] = p
        mixed = mixed + nn(p.astype(BF16), v * masks[h])
    mixed = mixed.astype(BF16)
    branch = nn(mixed, wproj[...]).astype(BF16)
    residual = tokens + branch.astype(F32)
    n2, xhat2, inv2 = norm(residual, gain2)
    pre = nn(n2, wup[...])
    square = pre * pre
    tanh = jnp.tanh(ROOT * (pre + COEFF * pre * square))
    hidden = (0.5 * pre * (1.0 + tanh)).astype(BF16)
    slope = 0.5 * (1.0 + tanh) + 0.5 * pre * (1.0 - tanh * tanh) * ROOT * (
        1.0 + 3.0 * COEFF * square
    )
    block = residual + nt(hidden, wdown[...])

    def leave(which, value, sem):
        rows_st[...] = value
        copies = []
        for half in range(2):
            for part in range(2):
                i = half * 2 + part
                for c in range(6):
                    row = (11 - part * 6 - c) * 16 + half * 8
                    side, column = c // 3, c % 3
                    ex_st[i, pl.ds(side * 8, 8), pl.ds(column * C, C)] = rows_st[pl.ds(row, 8), :]
                out = ex_s if i else ex_r
                out[which, i] = ex_st[i].astype(BF16)
                if i:
                    copies.append(
                        push(ex_s.at[which, i], ex_r.at[which, i], sem, i - 1, near(half, part))
                    )
        return copies

    exit_block = leave(0, block, s_exb)

    land(1, gs, entry2)
    grads = gs[...]
    grads16 = grads.astype(BF16)
    grad_pre = (nn(grads16, wdown[...]) * slope).astype(BF16)
    down = tn(grads16, hidden)
    up = tn(n2, grad_pre)

    def put(start, value, lanes=(0, 128)):
        value = value.astype(BF16)
        for src, group, piece, row, take in flat_pieces(per, start, value.shape[0]):
            bufs[group][piece, pl.ds(row, take), pl.ds(lanes[0], lanes[1] - lanes[0])] = value[
                src : src + take
            ]

    def half_to_core(buf, dst, sem, count):
        return push(buf.at[pl.ds((1 - core) * count, count)], dst, sem, 0, at_core())

    def own_half(buf, other, out, count, copy):
        copy.wait()
        for i in range(count):
            out[i] = (buf[core * count + i].astype(F32) + other[i].astype(F32)).astype(BF16)

    def far_first(count):
        return sorted(range(1, count), key=lambda j: -min(j, count - j))

    def deal(pieces, slots, sem, me, count, where):
        return [
            push(pieces(lax.rem(me + j, count)), slots.at[j - 1], sem, j - 1, where(j))
            for j in far_first(count)
        ]

    def share(ref, sem, count, where):
        return [push(ref, ref, sem, j - 1, where(j)) for j in far_first(count)]

    def sum_dealt(own, copies, slots):
        total = own.astype(F32)
        for copy in copies:
            copy.wait()
        for i in range(len(copies)):
            total = total + slots[i].astype(F32)
        return total.astype(BF16)

    def sum_shared(copies, slots, count):
        for copy in copies:
            copy.wait()
        total = slots[0].astype(F32)
        for i in range(1, count):
            total = total + slots[i].astype(F32)
        return total.astype(BF16)

    def pass_on(fin, copies, sem, me, count):
        passed = []
        for j, copy in reversed(list(zip(far_first(count), copies))):
            copy.wait()
            got = fin.at[core * count + lax.rem(me - j + count, count)]
            passed.append(push(got, got, sem, j, at_core()))
        return passed

    class Flat:
        def __init__(self, refs, sem, me, count, where, last, last_count, last_where):
            self.buf, self.c, self.m1, self.r2, self.x, self.z, self.fin = refs
            self.sem, self.me, self.count, self.where = sem, me, count, where
            self.last, self.last_count, self.last_where = last, last_count, last_where

        def start(self):
            self.copies = half_to_core(self.buf, self.c, self.sem[0], self.count)

        def deal(self):
            own_half(self.buf, self.c, self.m1, self.count, self.copies)
            self.copies = deal(
                lambda i: self.m1.at[i], self.r2, self.sem[1], self.me, self.count, self.where
            )

        def cross(self):
            self.x[x] = sum_dealt(self.m1[self.me], self.copies, self.r2)
            self.copies = share(self.x.at[x], self.sem[2], nx, at_x)

        def far(self):
            self.z[self.last] = sum_shared(self.copies, self.x, nx)
            self.copies = share(
                self.z.at[self.last], self.sem[3], self.last_count, self.last_where
            )

        def gather(self):
            own = self.fin.at[core * self.count + self.me]
            own[...] = sum_shared(self.copies, self.z, self.last_count)
            self.copies = share(own, self.sem[4], self.count, self.where)
            self.passed = [push(own, own, self.sem[5], 0, at_core())]

        def pass_on(self):
            self.passed += pass_on(self.fin, self.copies, self.sem[5], self.me, self.count)

        def wait(self):
            for copy in self.passed:
                copy.wait()

    ways = ((y, ny, at_y, z, nz, at_z), (z, nz, at_z, y, ny, at_y))
    early_y, early_z, late_y, late_z = [
        Flat(flat_refs[i], s_groups[7 + 6 * i : 13 + 6 * i], *ways[i % 2]) for i in range(4)
    ]

    for i in range(6):
        put(AT_UP + i * 192, up[:, i * 128 : (i + 1) * 128])
        put(AT_DOWN + i * 192, down[:, i * 128 : (i + 1) * 128])
    copies_a = half_to_core(buf_a, c_a, s_a[0], nx)
    early_y.start()

    grad_n2 = nt(grad_pre, wup[...])
    grad_in, norm2 = norm_back(grad_n2, xhat2, inv2, gain2)
    grad_res = grads + grad_in
    grad_branch = grad_res.astype(BF16)
    proj = tn(mixed, grad_branch)
    put(AT_PROJ, proj[:, :128])
    early_z.start()
    grad_mixed = nt(grad_branch, wproj[...]).astype(BF16)

    def piece_of(ref, index):
        size = per[0] // ny
        return ref.at[pl.ds(pl.multiple_of(index * size, 16), size)]

    dq = jnp.zeros((192, C), F32)
    dk = jnp.zeros((192, C), F32)
    dv = jnp.zeros((192, C), F32)
    for h in range(HEADS):
        gm = grad_mixed * masks[h]
        p = probs[h]
        dp = nt(gm, v)
        t = p * dp
        ds = ((t - p * jnp.sum(t, axis=-1, keepdims=True)) * SCALE).astype(BF16)
        zfold[h] = ds
        dv = dv + tn(p.astype(BF16), gm)
        dk = dk + tn(ds, q * masks[h])
        dq = dq + nn(ds, k * masks[h])
        if h == 2:
            own_half(buf_a, c_a, m1_a, nx, copies_a)
            copies_a = deal(lambda i: m1_a.at[i], r2_a, s_a[1], x, nx, at_x)
            early_y.deal()
        if h == 5:
            early_z.deal()
    grad_packed = jnp.concatenate([dq, dk, dv], axis=1).astype(BF16)
    qkv = tn(n1, grad_packed)
    grad_n1 = nt(grad_packed, wqkv[...])
    grad_in1, norm1 = norm_back(grad_n1, xhat1, inv1, gain1)

    for i in range(4):
        put(AT_QKV + i * 192, qkv[:, i * 128 : (i + 1) * 128])
    put(AT_REST, qkv[:, 512:], (0, 64))
    put(AT_REST, proj[:, 128:], (64, 128))
    nst[0:1, :] = norm1[:, :128]
    nst[1:2, 0:64] = norm1[:, 128:]
    nst[2:3, :] = norm2[:, :128]
    nst[3:4, 0:64] = norm2[:, 128:]
    put(AT_NORMS, nst[...])
    late_y.start()
    late_z.start()

    token_grad = grad_res + grad_in1.astype(BF16).astype(F32)
    exit_token = leave(1, token_grad, s_ext)

    def fold(h, carry):
        ds = zfold[h]
        ffold[...] = jnp.zeros_like(ffold)
        for bj in range(12):
            one = (iota((1, 192), 1) >> 4 == bj).astype(F32).astype(BF16)
            ffold[pl.ds((11 - bj) * 16, 192), :] += ds * one
        wide = nt(ffold[...], m2).reshape(23, 16, 144) * m1[None]
        fsum[h, 0:23, :] = jnp.sum(wide, axis=1) * (1.0 / SCALE)
        return carry

    lax.fori_loop(0, HEADS // 2, fold, 0)
    late_y.deal()
    late_z.deal()
    m2_a[...] = sum_dealt(m1_a[x], copies_a, r2_a)
    copies_a = deal(lambda i: piece_of(m2_a, i), r3_a, s_a[2], y, ny, at_y)
    early_y.cross()
    early_z.cross()
    lax.fori_loop(HEADS // 2, HEADS, fold, 0)
    for h in range(HEADS):
        bst[pl.ds(h * 24, 23), :] = fsum[h, 0:23, 0:128]
        bst[pl.ds(144, 23), pl.ds(h * 16, 16)] = fsum[h, 0:23, 128:144]
    rb = 256 // nz
    b_s[...] = bst[...].astype(BF16).reshape(nz, rb, 128)
    copies_bias = deal(lambda i: b_s.at[i], b_r1, s_b1, z, nz, at_z)

    z_a[z] = sum_dealt(piece_of(m2_a, y)[...], copies_a, r3_a)
    copies_a = share(z_a.at[z], s_a[3], nz, at_z)
    late_y.cross()
    late_z.cross()
    early_y.far()
    early_z.far()
    b_y[y_hi] = sum_dealt(b_s[z], copies_bias, b_r1)
    copies_bias = share(b_y.at[y_hi], s_b2, ny_hi, at_yhi)
    mine = core * nx + x
    done = piece_of(fin_a.at[mine], y)
    done[...] = sum_shared(copies_a, z_a, nz)
    copies_a = share(done, s_a[4], ny, at_y)
    late_y.far()
    late_z.far()
    early_y.gather()
    early_z.gather()
    b_fin[z] = sum_shared(copies_bias, b_y, ny_hi)
    copies_bias = share(b_fin.at[z], s_b3, nz, at_z)
    stores = []

    def store(*which):
        for i in which:
            copy = pltpu.make_async_copy(ready[i], outs[i], out_sem.at[i])
            copy.start()
            stores.append(copy)

    def arrive(which, copies, out):
        for copy in copies:
            copy.wait()
        for half in range(2):
            for part in range(2):
                i = (1 - half) * 2 + 1 - part
                rows = ex_r[which, i].astype(F32)
                for row in range(3):
                    for side in range(2):
                        place = pl.ds(part * HALF + side * 576, 576)
                        out[half * 3 + row, :, place] = rows[
                            side * 8 + row * 2 : side * 8 + row * 2 + 2, 0:576
                        ].astype(BF16)

    arrive(0, exit_block, o_block)
    arrive(1, exit_token, o_token)

    store(0, 1)
    late_y.gather()
    late_z.gather()
    for copy in copies_a:
        copy.wait()
    copies_a = share(fin_a.at[mine], s_a[5], nx, at_x)
    passed_a = [push(fin_a.at[mine], fin_a.at[mine], s_a[6], 0, at_core())]
    for copy in copies_bias:
        copy.wait()
    flat = b_fin[...].reshape(256, 128).astype(F32)
    for h in range(HEADS):
        o_bias[h, :, 0, 0:128] = flat[h * 24 : h * 24 + 23]
        o_bias[h, :, 0, 128:144] = flat[144:167, h * 16 : h * 16 + 16]
    store(5)
    early_y.pass_on()
    early_z.pass_on()
    passed_a += pass_on(fin_a, copies_a, s_a[6], x, nx)
    late_y.pass_on()
    late_z.pass_on()

    scale = float(cells) ** (-0.5)

    def take(start, rows):
        parts = [
            fins[group][piece, pl.ds(row, count), :]
            for _, group, piece, row, count in flat_pieces(per, start, rows)
        ]
        whole = parts[0] if len(parts) == 1 else jnp.concatenate(parts, axis=0)
        return whole.astype(F32) * scale

    early_y.wait()
    early_z.wait()
    for copy in passed_a:
        copy.wait()
    for i in range(6):
        o_up[:, pl.ds(i * 128, 128)] = take(AT_UP + i * 192, 192)
    store(7)
    for i in range(6):
        o_down[:, pl.ds(i * 128, 128)] = take(AT_DOWN + i * 192, 192)
    store(8)
    o_proj[:, 0:128] = take(AT_PROJ, 192)
    late_y.wait()
    late_z.wait()
    for i in range(4):
        o_qkv[:, pl.ds(i * 128, 128)] = take(AT_QKV + i * 192, 192)
    rest = take(AT_REST, 192)
    o_qkv[:, 512:576] = rest[:, :64]
    o_proj[:, 128:192] = rest[:, 64:]
    rest = take(AT_NORMS, 16)
    o_n1[:, 0:128] = rest[0:1, :]
    o_n1[:, 128:192] = rest[1:2, :64]
    o_n2[:, 0:128] = rest[2:3, :]
    o_n2[:, 128:192] = rest[3:4, :64]
    store(2, 3, 4, 6)
    for copy in stores:
        copy.wait()


def piece_rows(geo):
    nlat, nlon, ny_lo, nx, nz, ny_hi = geo
    counts = (nx, ny_lo * ny_hi, nz, ny_lo * ny_hi, nz)
    return tuple(rows // (2 * count) for rows, count in zip(ROWS, counts))


def spread(*refs):
    inputs, outs, held = refs[:9], refs[9:18], refs[18:27]
    sem_in, sem_out = refs[27:]
    order = (7, 8, 3, 5, 4, 0, 1, 2, 6)
    loads = [pltpu.make_async_copy(inputs[i], held[i], sem_in.at[i]) for i in range(9)]
    stores = [pltpu.make_async_copy(held[i], outs[i], sem_out.at[i]) for i in range(9)]
    for i in order:
        loads[i].start()
    for i in order:
        loads[i].wait()
        stores[i].start()
    for i in order:
        stores[i].wait()


def on_device(geo, tokens, labels, gain1, wqkv, wproj, table, gain2, wup, wdown, cotangent):
    nlat, nlon, ny_lo, nx, nz, ny_hi = geo
    ny = ny_lo * ny_hi
    pa, *flat_rows = piece_rows(geo)
    rb = 256 // nz
    vmem = pltpu.VMEM
    args = (
        tokens.transpose(1, 0, 2), labels.transpose(1, 0, 2), gain1.reshape(1, C), wqkv, wproj,
        table.transpose(1, 2, 0, 3), gain2.reshape(1, C), wup, wdown.T, cotangent.transpose(1, 0, 2),
    )
    shape = jax.ShapeDtypeStruct
    shapes = (
        shape((6, 2, 12 * C), BF16),
        shape((6, 2, 12 * C), BF16),
        shape((1, C), F32),
        shape((C, 3 * C), F32),
        shape((C, C), F32),
        shape((HEADS, 23, 1, 144), F32),
        shape((1, C), F32),
        shape((C, FFN), F32),
        shape((C, FFN), F32),
    )
    scratch = [vmem(arg.shape, arg.dtype) for arg in args + shapes]
    scratch += [
        vmem((2, 4, 16, HOLD), F32),
        vmem((2, 3, 16, HOLD), BF16),
        vmem((2, 3, 16, HOLD), BF16),
        vmem((192, C), F32),
        vmem((192, C), F32),
        vmem((16, 128), F32),
        vmem((368, 192), F32),
        vmem((HEADS, 192, 192), F32),
        vmem((HEADS, 192, 192), F32),
        vmem((4, 16, HOLD), F32),
        vmem((2, 4, 16, HOLD), BF16),
        vmem((2, 4, 16, HOLD), BF16),
        vmem((192, C), F32),
        vmem((16, 128), F32),
        vmem((HEADS, 192, 192), BF16),
        vmem((368, 192), BF16),
        vmem((HEADS, 24, 144), F32),
        vmem((256, 128), F32),
        vmem((nz, rb, 128), BF16),
        vmem((nz - 1, rb, 128), BF16),
        vmem((ny_hi, rb, 128), BF16),
        vmem((nz, rb, 128), BF16),
        vmem((2 * nx, pa, 128), BF16),
        vmem((nx, pa, 128), BF16),
        vmem((nx, pa, 128), BF16),
        vmem((nx - 1, pa, 128), BF16),
        vmem((pa, 128), BF16),
        vmem((ny - 1, pa // ny, 128), BF16),
        vmem((nz, pa // ny, 128), BF16),
        vmem((2 * nx, pa, 128), BF16),
    ]
    for piece, first, last in zip(flat_rows, (ny, nz, ny, nz), (nz, ny, nz, ny)):
        scratch += [
            vmem((2 * first, piece, 128), BF16),
            vmem((first, piece, 128), BF16),
            vmem((first, piece, 128), BF16),
            vmem((first - 1, piece, 128), BF16),
            vmem((nx, piece, 128), BF16),
            vmem((last, piece, 128), BF16),
            vmem((2 * first, piece, 128), BF16),
        ]
    scratch += [
        pltpu.SemaphoreType.DMA((10,)),
        pltpu.SemaphoreType.DMA((9,)),
    ]
    counts = [3, 3, 3, 3, nz - 1, ny_hi - 1, nz - 1]
    counts += [1, nx - 1, ny - 1, nz - 1, ny - 1, nx - 1, nx]
    for first, last in ((ny, nz), (nz, ny)) * 2:
        counts += [1, first - 1, nx - 1, last - 1, first - 1, first]
    for count in counts:
        scratch += [pltpu.SemaphoreType.DMA((count,)), pltpu.SemaphoreType.DMA((count,))]
    anywhere = pl.BlockSpec(memory_space=pl.ANY)
    out = pl.pallas_call(
        functools.partial(kernel, geo),
        out_shape=shapes,
        in_specs=[anywhere] * 10,
        out_specs=(anywhere,) * 9,
        scratch_shapes=scratch,
        compiler_params=pltpu.CompilerParams(
            collective_id=0, has_side_effects=True, vmem_limit_bytes=63 * 1024 * 1024
        ),
    )(*args)
    out = pl.pallas_call(
        spread,
        out_shape=shapes,
        in_specs=[anywhere] * 9,
        out_specs=(anywhere,) * 9,
        scratch_shapes=[vmem(each.shape, each.dtype) for each in shapes]
        + [pltpu.SemaphoreType.DMA((9,)), pltpu.SemaphoreType.DMA((9,))],
        compiler_params=pltpu.CompilerParams(vmem_limit_bytes=63 * 1024 * 1024),
    )(*out)
    block, token, norm1, qkv, proj, bias, norm2, up, down = out
    return (
        block.transpose(1, 0, 2), token.transpose(1, 0, 2), norm1.reshape(C), qkv, proj,
        bias.transpose(2, 0, 1, 3), norm2.reshape(C), up, down.T,
    )


def geometry(mesh):
    nlat, nlon = mesh.shape["lat"], mesh.shape["lon"]
    ny_hi = 4 if nlon == 32 else 2
    nx = min(4, nlat // 2)
    return nlat, nlon, nlat // 2 // nx, nx, nlon // ny_hi, ny_hi


def solution(mesh):
    cells, band = P(None, "lat", "lon"), P("lat", None, None, None)
    return jax.shard_map(
        functools.partial(on_device, geometry(mesh)),
        mesh=mesh,
        in_specs=(cells, cells, P(), P(), P(), band, P(), P(), P(), cells),
        out_specs=(cells, cells, P(), P(), P(), band, P(), P(), P()),
        check_vma=False,
    )
```

```python
import functools

import jax
import jax.numpy as jnp
from jax import lax
from jax.experimental import pallas as pl
from jax.experimental.pallas import tpu as pltpu
from jax.sharding import PartitionSpec as P

MESH = pl.DeviceIdType.MESH
F32, BF16 = jnp.float32, jnp.bfloat16
C, HEADS, FFN = 192, 6, 768
HALF = 6 * C
EPS = 1e-05
COEFF = 0.044715
ROOT = 0.7978845608028654
MASKED = -1e30
SCALE = 32.0**-0.5
ROWS = (1024, 768, 768, 512, 512)
AT_UP, AT_DOWN, AT_PROJ, AT_QKV, AT_REST, AT_NORMS = 0, 1152, 2304, 2560, 3328, 3520
HOLD = 640


def nn(a, b):
    return jnp.dot(a, b, preferred_element_type=F32)


def nt(a, b):
    return lax.dot_general(a, b, (((1,), (1,)), ((), ())), preferred_element_type=F32)


def tn(a, b):
    return lax.dot_general(a, b, (((0,), (0,)), ((), ())), preferred_element_type=F32)


def mean(x):
    return jnp.sum(x, axis=-1, keepdims=True) * (1.0 / C)


def norm(x, gain):
    center = x - mean(x)
    inv = lax.rsqrt(mean(center * center) + EPS)
    xhat = center * inv
    return (xhat * gain).astype(BF16), xhat, inv


def norm_back(grad, xhat, inv, gain):
    g = grad * gain
    grad_in = inv * (g - mean(g) - xhat * mean(g * xhat))
    return grad_in, jnp.sum(grad * xhat, axis=0, keepdims=True)


def iota(shape, dim):
    return lax.broadcasted_iota(jnp.int32, shape, dim)


def cell_row(rho):
    half, r = rho >> 3, rho & 7
    return (r & 1) * 6 + half * 3 + (r >> 1), r < 6


def flat_pieces(sizes, start, rows):
    at = start
    while at < start + rows:
        group, base = 0, 0
        while at >= base + ROWS[group]:
            base += ROWS[group]
            group += 1
        per = sizes[group]
        inside = at - base
        take = min(per - inside % per, start + rows - at)
        yield at - start, group, inside // per, inside % per, take
        at += take


def kernel(
    geo, *refs,
):
    inputs, outs, held, ready, refs = refs[:10], refs[10:19], refs[19:29], refs[29:38], refs[38:]
    tok, lab, g1, wqkv, wproj, btab, g2, wup, wdown, cot = held
    o_block, o_token, o_n1, o_qkv, o_proj, o_bias, o_n2, o_up, o_down = ready
    (
        stage, ent_s, ent_r, xs, gs, labs, ytab, bias, probs, ex_st, ex_s, ex_r, rows_st,
        nst, zfold, ffold, fsum, bst, b_s, b_r1, b_y, b_fin,
        buf_a, c_a, m1_a, r2_a, m2_a, r3_a, z_a, fin_a, *flat_refs,
    ) = refs[:58]
    in_sem, out_sem, *sems = refs[58:]
    nlat, nlon, ny_lo, nx, nz, ny_hi = geo
    ny = ny_lo * ny_hi
    per = piece_rows(geo)
    flat_refs = [flat_refs[7 * i : 7 * i + 7] for i in range(4)]
    bufs = (buf_a, *(each[0] for each in flat_refs))
    fins = (fin_a, *(each[6] for each in flat_refs))
    cells = 144 * nlat * nlon
    s_ent, s_ent2, s_exb, s_ext, s_b1, s_b2, s_b3, *s_groups = [
        (sems[2 * i], sems[2 * i + 1]) for i in range(len(sems) // 2)
    ]
    s_a = s_groups[:7]

    lat, lon = lax.axis_index("lat"), lax.axis_index("lon")
    core = lax.rem(lat, 2)
    x = lax.rem(lat // 2, nx)
    y_lo = lat // (2 * nx)
    z = lon // ny_hi
    y_hi = lax.rem(lon, ny_hi)
    y = y_hi * ny_lo + y_lo

    def at_core():
        return (lat + 1 - 2 * core, lon)

    def at_x(k):
        return ((y_lo * nx + lax.rem(x + k, nx)) * 2 + core, lon)

    def at_y(k):
        other = lax.rem(y + k, ny)
        return ((lax.rem(other, ny_lo) * nx + x) * 2 + core, z * ny_hi + other // ny_lo)

    def at_yhi(k):
        return (lat, z * ny_hi + lax.rem(y_hi + k, ny_hi))

    def at_z(k):
        return (lat, lax.rem(z + k, nz) * ny_hi + y_hi)

    def near(da, db):
        return (lax.rem(lat + da + nlat, nlat), lax.rem(lon + db + nlon, nlon))

    def push(src, dst, sem, i, dev):
        copy = pltpu.make_async_remote_copy(
            src_ref=src, dst_ref=dst, send_sem=sem[0].at[i], recv_sem=sem[1].at[i],
            device_id=dev, device_id_type=MESH,
        )
        copy.start()
        return copy

    barrier = pltpu.get_barrier_semaphore()
    partners = [near(-1, 0), near(0, -1), near(-1, -1), near(1, 0), near(0, 1), near(1, 1)]
    partners += [at_core()]
    partners += [at_x(k) for k in range(1, nx)]
    partners += [at_y(k) for k in range(1, ny)]
    partners += [at_z(k) for k in range(1, nz)]
    for dev in partners:
        pl.semaphore_signal(barrier, inc=1, device_id=dev, device_id_type=MESH)
    loads = {}
    for i in (0, 9, 1, 5, 2, 3, 4, 6, 7, 8):
        loads[i] = pltpu.make_async_copy(inputs[i], held[i], in_sem.at[i])
        loads[i].start()

    loads[0].wait()

    stage[...] = jnp.zeros_like(stage)
    ex_st[...] = jnp.zeros_like(ex_st)

    def quarters(kind, ref):
        for half in range(2):
            for part in range(2):
                for row in range(3):
                    for side in range(2):
                        stage[kind, half * 2 + part, pl.ds(side * 8 + row * 2, 2), 0:576] = ref[
                            half * 3 + row, :, pl.ds(part * HALF + side * 576, 576)
                        ].astype(F32)
        for i in range(3):
            ent_s[kind, i] = stage[kind, i].astype(BF16)

    quarters(0, tok)
    pl.semaphore_wait(barrier, len(partners))
    places = ((0, 0), (0, 1), (1, 0))

    def enter(kind, sem):
        return [
            push(ent_s.at[kind, i], ent_r.at[kind, i], sem, i, near(half - 1, part - 1))
            for i, (half, part) in enumerate(places)
        ]

    entry = enter(0, s_ent)
    loads[1].wait()
    loads[5].wait()

    labs[...] = jnp.full_like(labs, -1.0)
    for half in range(2):
        for row in range(3):
            labs[pl.ds(half * 8 + row * 2, 2), pl.ds(0, 12)] = lab[half * 3 + row].astype(F32)
    lab16 = labs[...].astype(BF16)
    pick = (11 - (iota((192, 128), 0) >> 4) == iota((192, 128), 1)).astype(F32).astype(BF16)
    lane_all = nt(lab16, pick)
    lane_lab = jnp.sum(
        jnp.where(iota((16, 192), 0) == (iota((16, 192), 1) & 15), lane_all, 0.0),
        axis=0, keepdims=True,
    )
    row_all = nt(pick, lab16)
    row_lab = jnp.sum(
        jnp.where(iota((192, 16), 1) == (iota((192, 16), 0) & 15), row_all, 0.0),
        axis=1, keepdims=True,
    )
    same = row_lab == lane_lab

    place, real = cell_row(iota((16, 144), 0))
    spot = iota((16, 144), 1)
    spot_row = (spot * 171) >> 11
    m1 = jnp.where((spot_row == place) & real, 1.0, 0.0)
    place_j, real_j = cell_row(iota((144, 192), 1) & 15)
    spot_j = iota((144, 192), 0)
    spot_col = spot_j - ((spot_j * 171) >> 11) * 12
    m2 = jnp.where((spot_col == place_j) & real_j, 1.0, 0.0).astype(BF16)
    group = iota((192, 192), 1) >> 4

    def build(h, carry):
        left = btab[h]
        full = jnp.zeros((368, 192), F32)
        for _ in range(3):
            piece = left.astype(BF16).astype(F32)
            left = left - piece
            wide = (piece * m1[None]).reshape(368, 144)
            full = full + nn(wide.astype(BF16), m2)
        ytab[...] = full
        out = ytab[pl.ds(176, 192), :]
        for bj in range(1, 12):
            out = jnp.where(group == bj, ytab[pl.ds((11 - bj) * 16, 192), :], out)
        bias[h] = jnp.where(same, out, MASKED)
        return carry

    lax.fori_loop(0, HEADS // 2, build, 0)
    loads[9].wait()
    quarters(1, cot)
    entry2 = enter(1, s_ent2)
    lax.fori_loop(HEADS // 2, HEADS, build, 0)
    for i in (2, 4):
        bufs[i][...] = jnp.zeros_like(bufs[i])
    nst[...] = jnp.zeros_like(nst)
    bst[...] = jnp.zeros_like(bst)

    def lay(out, quarter, half, part):
        for c in range(6):
            row = (11 - part * 6 - c) * 16 + half * 8
            side, column = c // 3, c % 3
            out[pl.ds(row, 8), :] = quarter[side * 8 : side * 8 + 8, column * C : (column + 1) * C]

    def land(kind, out, copies):
        lay(out, stage[kind, 3], 0, 0)
        for i, (half, part) in enumerate(places):
            copies[i].wait()
            lay(out, ent_r[kind, i].astype(F32), 1 - half, 1 - part)

    for i in (2, 3, 4, 6, 7, 8):
        loads[i].wait()
    land(0, xs, entry)

    gain1, gain2 = g1[...], g2[...]
    tokens = xs[...]
    n1, xhat1, inv1 = norm(tokens, gain1)
    packed = nn(n1, wqkv[...]).astype(BF16)
    q, k, v = packed[:, :C], packed[:, C : 2 * C], packed[:, 2 * C :]
    head_of = iota((1, C), 1) >> 5
    masks = [(head_of == h).astype(F32).astype(BF16) for h in range(HEADS)]
    mixed = jnp.zeros((192, C), F32)
    for h in range(HEADS):
        s = nt(q * masks[h], k) * SCALE + bias[h]
        e = jnp.exp(s - jnp.max(s, axis=-1, keepdims=True))
        p = e * (1.0 / jnp.sum(e, axis=-1, keepdims=True))
        probs[h] = p
        mixed = mixed + nn(p.astype(BF16), v * masks[h])
    mixed = mixed.astype(BF16)
    branch = nn(mixed, wproj[...]).astype(BF16)
    residual = tokens + branch.astype(F32)
    n2, xhat2, inv2 = norm(residual, gain2)
    pre = nn(n2, wup[...])
    square = pre * pre
    tanh = jnp.tanh(ROOT * (pre + COEFF * pre * square))
    hidden = (0.5 * pre * (1.0 + tanh)).astype(BF16)
    slope = 0.5 * (1.0 + tanh) + 0.5 * pre * (1.0 - tanh * tanh) * ROOT * (
        1.0 + 3.0 * COEFF * square
    )
    block = residual + nt(hidden, wdown[...])

    def leave(which, value, sem):
        rows_st[...] = value
        copies = []
        for half in range(2):
            for part in range(2):
                i = half * 2 + part
                for c in range(6):
                    row = (11 - part * 6 - c) * 16 + half * 8
                    side, column = c // 3, c % 3
                    ex_st[i, pl.ds(side * 8, 8), pl.ds(column * C, C)] = rows_st[pl.ds(row, 8), :]
                out = ex_s if i else ex_r
                out[which, i] = ex_st[i].astype(BF16)
                if i:
                    copies.append(
                        push(ex_s.at[which, i], ex_r.at[which, i], sem, i - 1, near(half, part))
                    )
        return copies

    exit_block = leave(0, block, s_exb)

    land(1, gs, entry2)
    grads = gs[...]
    grads16 = grads.astype(BF16)
    grad_pre = (nn(grads16, wdown[...]) * slope).astype(BF16)
    down = tn(grads16, hidden)
    up = tn(n2, grad_pre)

    def put(start, value, lanes=(0, 128)):
        value = value.astype(BF16)
        for src, group, piece, row, take in flat_pieces(per, start, value.shape[0]):
            bufs[group][piece, pl.ds(row, take), pl.ds(lanes[0], lanes[1] - lanes[0])] = value[
                src : src + take
            ]

    def half_to_core(buf, dst, sem, count):
        return push(buf.at[pl.ds((1 - core) * count, count)], dst, sem, 0, at_core())

    def own_half(buf, other, out, count, copy):
        copy.wait()
        for i in range(count):
            out[i] = (buf[core * count + i].astype(F32) + other[i].astype(F32)).astype(BF16)

    def far_first(count):
        return sorted(range(1, count), key=lambda j: -min(j, count - j))

    def deal(pieces, slots, sem, me, count, where):
        return [
            push(pieces(lax.rem(me + j, count)), slots.at[j - 1], sem, j - 1, where(j))
            for j in far_first(count)
        ]

    def share(ref, sem, count, where):
        return [push(ref, ref, sem, j - 1, where(j)) for j in far_first(count)]

    def sum_dealt(own, copies, slots):
        total = own.astype(F32)
        for copy in copies:
            copy.wait()
        for i in range(len(copies)):
            total = total + slots[i].astype(F32)
        return total.astype(BF16)

    def sum_shared(copies, slots, count):
        for copy in copies:
            copy.wait()
        total = slots[0].astype(F32)
        for i in range(1, count):
            total = total + slots[i].astype(F32)
        return total.astype(BF16)

    def pass_on(fin, copies, sem, me, count):
        passed = []
        for j, copy in reversed(list(zip(far_first(count), copies))):
            copy.wait()
            got = fin.at[core * count + lax.rem(me - j + count, count)]
            passed.append(push(got, got, sem, j, at_core()))
        return passed

    class Flat:
        def __init__(self, refs, sem, me, count, where, last, last_count, last_where):
            self.buf, self.c, self.m1, self.r2, self.x, self.z, self.fin = refs
            self.sem, self.me, self.count, self.where = sem, me, count, where
            self.last, self.last_count, self.last_where = last, last_count, last_where

        def start(self):
            self.copies = half_to_core(self.buf, self.c, self.sem[0], self.count)

        def deal(self):
            own_half(self.buf, self.c, self.m1, self.count, self.copies)
            self.copies = deal(
                lambda i: self.m1.at[i], self.r2, self.sem[1], self.me, self.count, self.where
            )

        def cross(self):
            self.x[x] = sum_dealt(self.m1[self.me], self.copies, self.r2)
            self.copies = share(self.x.at[x], self.sem[2], nx, at_x)

        def far(self):
            self.z[self.last] = sum_shared(self.copies, self.x, nx)
            self.copies = share(
                self.z.at[self.last], self.sem[3], self.last_count, self.last_where
            )

        def gather(self):
            own = self.fin.at[core * self.count + self.me]
            own[...] = sum_shared(self.copies, self.z, self.last_count)
            self.copies = share(own, self.sem[4], self.count, self.where)
            self.passed = [push(own, own, self.sem[5], 0, at_core())]

        def pass_on(self):
            self.passed += pass_on(self.fin, self.copies, self.sem[5], self.me, self.count)

        def wait(self):
            for copy in self.passed:
                copy.wait()

    ways = ((y, ny, at_y, z, nz, at_z), (z, nz, at_z, y, ny, at_y))
    early_y, early_z, late_y, late_z = [
        Flat(flat_refs[i], s_groups[7 + 6 * i : 13 + 6 * i], *ways[i % 2]) for i in range(4)
    ]

    for i in range(6):
        put(AT_UP + i * 192, up[:, i * 128 : (i + 1) * 128])
        put(AT_DOWN + i * 192, down[:, i * 128 : (i + 1) * 128])
    copies_a = half_to_core(buf_a, c_a, s_a[0], nx)
    early_y.start()

    grad_n2 = nt(grad_pre, wup[...])
    grad_in, norm2 = norm_back(grad_n2, xhat2, inv2, gain2)
    grad_res = grads + grad_in
    grad_branch = grad_res.astype(BF16)
    proj = tn(mixed, grad_branch)
    put(AT_PROJ, proj[:, :128])
    early_z.start()
    grad_mixed = nt(grad_branch, wproj[...]).astype(BF16)

    def piece_of(ref, index):
        size = per[0] // ny
        return ref.at[pl.ds(pl.multiple_of(index * size, 16), size)]

    dq = jnp.zeros((192, C), F32)
    dk = jnp.zeros((192, C), F32)
    dv = jnp.zeros((192, C), F32)
    for h in range(HEADS):
        gm = grad_mixed * masks[h]
        p = probs[h]
        dp = nt(gm, v)
        t = p * dp
        ds = ((t - p * jnp.sum(t, axis=-1, keepdims=True)) * SCALE).astype(BF16)
        zfold[h] = ds
        dv = dv + tn(p.astype(BF16), gm)
        dk = dk + tn(ds, q * masks[h])
        dq = dq + nn(ds, k * masks[h])
        if h == 2:
            own_half(buf_a, c_a, m1_a, nx, copies_a)
            copies_a = deal(lambda i: m1_a.at[i], r2_a, s_a[1], x, nx, at_x)
            early_y.deal()
        if h == 5:
            early_z.deal()
    grad_packed = jnp.concatenate([dq, dk, dv], axis=1).astype(BF16)
    qkv = tn(n1, grad_packed)
    grad_n1 = nt(grad_packed, wqkv[...])
    grad_in1, norm1 = norm_back(grad_n1, xhat1, inv1, gain1)

    for i in range(4):
        put(AT_QKV + i * 192, qkv[:, i * 128 : (i + 1) * 128])
    put(AT_REST, qkv[:, 512:], (0, 64))
    put(AT_REST, proj[:, 128:], (64, 128))
    nst[0:1, :] = norm1[:, :128]
    nst[1:2, 0:64] = norm1[:, 128:]
    nst[2:3, :] = norm2[:, :128]
    nst[3:4, 0:64] = norm2[:, 128:]
    put(AT_NORMS, nst[...])
    late_y.start()
    late_z.start()

    token_grad = grad_res + grad_in1.astype(BF16).astype(F32)
    exit_token = leave(1, token_grad, s_ext)

    def fold(h, carry):
        ds = zfold[h]
        ffold[...] = jnp.zeros_like(ffold)
        for bj in range(12):
            one = (iota((1, 192), 1) >> 4 == bj).astype(F32).astype(BF16)
            ffold[pl.ds((11 - bj) * 16, 192), :] += ds * one
        wide = nt(ffold[...], m2).reshape(23, 16, 144) * m1[None]
        fsum[h, 0:23, :] = jnp.sum(wide, axis=1) * (1.0 / SCALE)
        return carry

    lax.fori_loop(0, 1, fold, 0)
    late_y.deal()
    late_z.deal()
    m2_a[...] = sum_dealt(m1_a[x], copies_a, r2_a)
    copies_a = deal(lambda i: piece_of(m2_a, i), r3_a, s_a[2], y, ny, at_y)
    early_y.cross()
    early_z.cross()
    lax.fori_loop(1, HEADS, fold, 0)
    for h in range(HEADS):
        bst[pl.ds(h * 24, 23), :] = fsum[h, 0:23, 0:128]
        bst[pl.ds(144, 23), pl.ds(h * 16, 16)] = fsum[h, 0:23, 128:144]
    rb = 256 // nz
    b_s[...] = bst[...].astype(BF16).reshape(nz, rb, 128)
    copies_bias = deal(lambda i: b_s.at[i], b_r1, s_b1, z, nz, at_z)

    z_a[z] = sum_dealt(piece_of(m2_a, y)[...], copies_a, r3_a)
    copies_a = share(z_a.at[z], s_a[3], nz, at_z)
    late_y.cross()
    late_z.cross()
    early_y.far()
    early_z.far()
    b_y[y_hi] = sum_dealt(b_s[z], copies_bias, b_r1)
    copies_bias = share(b_y.at[y_hi], s_b2, ny_hi, at_yhi)
    mine = core * nx + x
    done = piece_of(fin_a.at[mine], y)
    done[...] = sum_shared(copies_a, z_a, nz)
    copies_a = share(done, s_a[4], ny, at_y)
    late_y.far()
    late_z.far()
    early_y.gather()
    early_z.gather()
    b_fin[z] = sum_shared(copies_bias, b_y, ny_hi)
    copies_bias = share(b_fin.at[z], s_b3, nz, at_z)
    stores = []

    def store(*which):
        for i in which:
            copy = pltpu.make_async_copy(ready[i], outs[i], out_sem.at[i])
            copy.start()
            stores.append(copy)

    def arrive(which, copies, out):
        for copy in copies:
            copy.wait()
        for half in range(2):
            for part in range(2):
                i = (1 - half) * 2 + 1 - part
                rows = ex_r[which, i].astype(F32)
                for row in range(3):
                    for side in range(2):
                        place = pl.ds(part * HALF + side * 576, 576)
                        out[half * 3 + row, :, place] = rows[
                            side * 8 + row * 2 : side * 8 + row * 2 + 2, 0:576
                        ].astype(BF16)

    arrive(0, exit_block, o_block)
    arrive(1, exit_token, o_token)

    store(0, 1)
    late_y.gather()
    late_z.gather()
    for copy in copies_a:
        copy.wait()
    copies_a = share(fin_a.at[mine], s_a[5], nx, at_x)
    passed_a = [push(fin_a.at[mine], fin_a.at[mine], s_a[6], 0, at_core())]
    for copy in copies_bias:
        copy.wait()
    flat = b_fin[...].reshape(256, 128).astype(F32)
    for h in range(HEADS):
        o_bias[h, :, 0, 0:128] = flat[h * 24 : h * 24 + 23]
        o_bias[h, :, 0, 128:144] = flat[144:167, h * 16 : h * 16 + 16]
    store(5)
    early_y.pass_on()
    early_z.pass_on()
    passed_a += pass_on(fin_a, copies_a, s_a[6], x, nx)
    late_y.pass_on()
    late_z.pass_on()

    scale = float(cells) ** (-0.5)

    def take(start, rows):
        parts = [
            fins[group][piece, pl.ds(row, count), :]
            for _, group, piece, row, count in flat_pieces(per, start, rows)
        ]
        whole = parts[0] if len(parts) == 1 else jnp.concatenate(parts, axis=0)
        return whole.astype(F32) * scale

    early_y.wait()
    early_z.wait()
    for copy in passed_a:
        copy.wait()
    for i in range(6):
        o_up[:, pl.ds(i * 128, 128)] = take(AT_UP + i * 192, 192)
    store(7)
    for i in range(6):
        o_down[:, pl.ds(i * 128, 128)] = take(AT_DOWN + i * 192, 192)
    store(8)
    o_proj[:, 0:128] = take(AT_PROJ, 192)
    late_y.wait()
    late_z.wait()
    for i in range(4):
        o_qkv[:, pl.ds(i * 128, 128)] = take(AT_QKV + i * 192, 192)
    rest = take(AT_REST, 192)
    o_qkv[:, 512:576] = rest[:, :64]
    o_proj[:, 128:192] = rest[:, 64:]
    rest = take(AT_NORMS, 16)
    o_n1[:, 0:128] = rest[0:1, :]
    o_n1[:, 128:192] = rest[1:2, :64]
    o_n2[:, 0:128] = rest[2:3, :]
    o_n2[:, 128:192] = rest[3:4, :64]
    store(2, 3, 4, 6)
    for copy in stores:
        copy.wait()


def piece_rows(geo):
    nlat, nlon, ny_lo, nx, nz, ny_hi = geo
    counts = (nx, ny_lo * ny_hi, nz, ny_lo * ny_hi, nz)
    return tuple(rows // (2 * count) for rows, count in zip(ROWS, counts))


def spread(*refs):
    inputs, outs, held = refs[:9], refs[9:18], refs[18:27]
    sem_in, sem_out = refs[27:]
    order = (7, 8, 3, 5, 4, 0, 1, 2, 6)
    loads = [pltpu.make_async_copy(inputs[i], held[i], sem_in.at[i]) for i in range(9)]
    stores = [pltpu.make_async_copy(held[i], outs[i], sem_out.at[i]) for i in range(9)]
    for i in order:
        loads[i].start()
    for i in order:
        loads[i].wait()
        stores[i].start()
    for i in order:
        stores[i].wait()


def on_device(geo, tokens, labels, gain1, wqkv, wproj, table, gain2, wup, wdown, cotangent):
    nlat, nlon, ny_lo, nx, nz, ny_hi = geo
    ny = ny_lo * ny_hi
    pa, *flat_rows = piece_rows(geo)
    rb = 256 // nz
    vmem = pltpu.VMEM
    args = (
        tokens.transpose(1, 0, 2), labels.transpose(1, 0, 2), gain1.reshape(1, C), wqkv, wproj,
        table.transpose(1, 2, 0, 3), gain2.reshape(1, C), wup, wdown.T, cotangent.transpose(1, 0, 2),
    )
    shape = jax.ShapeDtypeStruct
    shapes = (
        shape((6, 2, 12 * C), BF16),
        shape((6, 2, 12 * C), BF16),
        shape((1, C), F32),
        shape((C, 3 * C), F32),
        shape((C, C), F32),
        shape((HEADS, 23, 1, 144), F32),
        shape((1, C), F32),
        shape((C, FFN), F32),
        shape((C, FFN), F32),
    )
    scratch = [vmem(arg.shape, arg.dtype) for arg in args + shapes]
    scratch += [
        vmem((2, 4, 16, HOLD), F32),
        vmem((2, 3, 16, HOLD), BF16),
        vmem((2, 3, 16, HOLD), BF16),
        vmem((192, C), F32),
        vmem((192, C), F32),
        vmem((16, 128), F32),
        vmem((368, 192), F32),
        vmem((HEADS, 192, 192), F32),
        vmem((HEADS, 192, 192), F32),
        vmem((4, 16, HOLD), F32),
        vmem((2, 4, 16, HOLD), BF16),
        vmem((2, 4, 16, HOLD), BF16),
        vmem((192, C), F32),
        vmem((16, 128), F32),
        vmem((HEADS, 192, 192), BF16),
        vmem((368, 192), BF16),
        vmem((HEADS, 24, 144), F32),
        vmem((256, 128), F32),
        vmem((nz, rb, 128), BF16),
        vmem((nz - 1, rb, 128), BF16),
        vmem((ny_hi, rb, 128), BF16),
        vmem((nz, rb, 128), BF16),
        vmem((2 * nx, pa, 128), BF16),
        vmem((nx, pa, 128), BF16),
        vmem((nx, pa, 128), BF16),
        vmem((nx - 1, pa, 128), BF16),
        vmem((pa, 128), BF16),
        vmem((ny - 1, pa // ny, 128), BF16),
        vmem((nz, pa // ny, 128), BF16),
        vmem((2 * nx, pa, 128), BF16),
    ]
    for piece, first, last in zip(flat_rows, (ny, nz, ny, nz), (nz, ny, nz, ny)):
        scratch += [
            vmem((2 * first, piece, 128), BF16),
            vmem((first, piece, 128), BF16),
            vmem((first, piece, 128), BF16),
            vmem((first - 1, piece, 128), BF16),
            vmem((nx, piece, 128), BF16),
            vmem((last, piece, 128), BF16),
            vmem((2 * first, piece, 128), BF16),
        ]
    scratch += [
        pltpu.SemaphoreType.DMA((10,)),
        pltpu.SemaphoreType.DMA((9,)),
    ]
    counts = [3, 3, 3, 3, nz - 1, ny_hi - 1, nz - 1]
    counts += [1, nx - 1, ny - 1, nz - 1, ny - 1, nx - 1, nx]
    for first, last in ((ny, nz), (nz, ny)) * 2:
        counts += [1, first - 1, nx - 1, last - 1, first - 1, first]
    for count in counts:
        scratch += [pltpu.SemaphoreType.DMA((count,)), pltpu.SemaphoreType.DMA((count,))]
    anywhere = pl.BlockSpec(memory_space=pl.ANY)
    out = pl.pallas_call(
        functools.partial(kernel, geo),
        out_shape=shapes,
        in_specs=[anywhere] * 10,
        out_specs=(anywhere,) * 9,
        scratch_shapes=scratch,
        compiler_params=pltpu.CompilerParams(
            collective_id=0, has_side_effects=True, vmem_limit_bytes=63 * 1024 * 1024
        ),
    )(*args)
    out = pl.pallas_call(
        spread,
        out_shape=shapes,
        in_specs=[anywhere] * 9,
        out_specs=(anywhere,) * 9,
        scratch_shapes=[vmem(each.shape, each.dtype) for each in shapes]
        + [pltpu.SemaphoreType.DMA((9,)), pltpu.SemaphoreType.DMA((9,))],
        compiler_params=pltpu.CompilerParams(vmem_limit_bytes=63 * 1024 * 1024),
    )(*out)
    block, token, norm1, qkv, proj, bias, norm2, up, down = out
    return (
        block.transpose(1, 0, 2), token.transpose(1, 0, 2), norm1.reshape(C), qkv, proj,
        bias.transpose(2, 0, 1, 3), norm2.reshape(C), up, down.T,
    )


def geometry(mesh):
    nlat, nlon = mesh.shape["lat"], mesh.shape["lon"]
    ny_hi = 4 if nlon == 32 else 2
    nx = min(4, nlat // 2)
    return nlat, nlon, nlat // 2 // nx, nx, nlon // ny_hi, ny_hi


def solution(mesh):
    cells, band = P(None, "lat", "lon"), P("lat", None, None, None)
    return jax.shard_map(
        functools.partial(on_device, geometry(mesh)),
        mesh=mesh,
        in_specs=(cells, cells, P(), P(), P(), band, P(), P(), P(), cells),
        out_specs=(cells, cells, P(), P(), P(), band, P(), P(), P()),
        check_vma=False,
    )
```
